512 devices in a mesh: tensor: 16 (over z), adapter: 32 (over y, x, core).
Axes of the slice: x: 4, y: 4, z: 16, core: 2. Of those that a mesh axis runs over, the one named last changes fastest.
Arguments:
- tokens: bfloat16 [8192, 8192], P('adapter', 'tensor'), may hold values from -6 to 6
- token_adapter_index: int32 [8192, 1], P('adapter'), may hold values from 0 to 127; in each aligned block of 256 rows (0 to 255, 256 to 511, ...) at most 8 rows name the same one
- adapter_table_row: int32 [128], replicated, may hold values from 0 to 127, each once
- key_value_weight: bfloat16 [8192, 2048], P('tensor'), may hold values from -0.09375 to 0.09375
- adapter_down_weight: bfloat16 [128, 8192, 128], P('adapter', 'tensor'), may hold values from -0.0625 to 0.0625
- adapter_up_weight: bfloat16 [128, 64, 2048], P('adapter'), may hold values from -0.75 to 0.75
Outputs:
- keys_values: bfloat16 [8192, 2048], P('adapter', 'tensor')
The draws below stay inside these ranges and needn't reach their ends.
Inputs may be any that keep to these rules, and one draw needn't show every extreme that they name: `token_adapter_index`: among the 256 rows of one aligned block (one device along adapter), no adapter is named more than 8 times, a bound that some block reaches. `adapter_table_row`: each value once.
All inputs are finite; a program needn't handle non-finite values.
Results may differ from the reference program's by a relative error of at most 0.0035.
Values may be sent and summed in bfloat16 or wider, within the bound.
A program may use at most 64 MiB of HBM per device.

```python
import math
import jax
import jax.numpy as jnp
import numpy as np
from jax import lax

MODEL_WIDTH = 8192
KVH = 8
HD = 128
ADAPTER_RANK = 64
TOK_DEV = 256
ADAPTER_COUNT = 128
CAP = 8
TOKENS = 8192
COLUMN_COUNT = 2048
N_ADAPTER = 32


def with_spikes(entries, own_key, source, target, shards_of, factor):
    def block_of(position):
        return (jnp.arange(entries.shape[position]) // (entries.shape[position] // shards_of)).reshape((-1,) + (1,) * (entries.ndim - 1 - position))

    one_side = jax.random.permutation(own_key, shards_of)[block_of(target)]
    second = (block_of(target) + shards_of // 2) % shards_of
    return jnp.where((block_of(source) == one_side) | (block_of(source) == second), factor * entries, entries)


def level_of(key, dims, split, smallest, largest):
    level, own = 1.0, jax.random.fold_in(key, 6)
    for dim, shards_of in split:
        steps = jnp.exp(jax.random.uniform(jax.random.fold_in(own, dim), (shards_of,), jnp.float32, smallest / len(split), largest / len(split)))
        level = level * jnp.repeat(steps, dims[dim] // shards_of).reshape([-1 if axis == dim else 1 for axis in range(len(dims))])
    return level


def routed_block(rng, own, number, rows, count, top, bound, lean):
    sequence = jax.random.permutation(rng, count)
    heavy_load, common = shares(count, rows * top, bound, lean, True), shares(count, rows * top, bound, lean, False)
    places = jnp.arange(count)

    def named(sizes, turn):
        used = int((sizes > 0).sum())
        fixed = max(1, used // 4)
        moved = fixed + (places - fixed + turn * (used - fixed)) % max(1, count - fixed)
        return jnp.zeros((count,), jnp.int32).at[sequence[jnp.where(places < fixed, places, moved)]].set(jnp.asarray(sizes, jnp.int32))

    sizes = jnp.where(number % 4 == 0, named(heavy_load, number // 4), named(common, number - number // 4 - 1))
    mixed = jax.random.permutation(jax.random.fold_in(own, 3), count)
    giver, receiver = mixed[0:count // 2 * 2:2], mixed[1:count // 2 * 2:2]
    room = jnp.minimum(sizes[giver] - 1, bound - sizes[receiver]) // 2
    room = jnp.where((giver == sequence[0]) | (receiver == sequence[0]) | (sizes[receiver] == 0), 0, jnp.maximum(room, 0))
    moved = jax.random.randint(jax.random.fold_in(own, 4), (count // 2,), 0, 1 << 20) % (room + 1)
    sizes = sizes.at[giver].add(-moved).at[receiver].add(moved)
    labels = jnp.searchsorted(jnp.cumsum(sizes), jnp.arange(rows * top), side="right").astype(jnp.int32)
    listing = labels.reshape(top, rows).T
    listing = listing[jax.random.permutation(jax.random.fold_in(own, 1), rows)]
    turn = jax.random.randint(jax.random.fold_in(own, 2), (rows, 1), 0, top)
    return jnp.take_along_axis(listing, (jnp.arange(top)[None, :] + turn) % top, axis=1)


def shares(amount, total, most, slope, full):
    weights = [(1 << 20) // math.isqrt(rank ** slope) + 1 for rank in range(1, amount + 1)]
    largest = most if full else min(most, max(-(-total // amount), total * weights[0] // sum(weights)))
    least = 1 if total - largest >= amount - 1 else 0
    given, spare = [largest] + [least] * (amount - 1), total - largest - least * (amount - 1)
    while spare > 0:
        candidates = [i for i in range(1, amount) if given[i] < largest] or [i for i in range(1, amount) if given[i] < most]
        pool, left = sum([weights[i] for i in candidates]), spare
        for i in candidates:
            addition = min(most - given[i], max(1, left * weights[i] // pool), spare)
            given[i] = given[i] + addition
            spare = spare - addition
    return np.array(given)


def scatter_about(own_key, shape, spread, bound, pieces=(), kind=jnp.bfloat16):
    gain = level_of(own_key, shape, pieces, -0.22, 0.18) if pieces else 1.0
    drawn = jax.random.normal(own_key, shape, jnp.float32) * spread * gain
    return jnp.minimum(jnp.maximum(drawn, -bound), bound).astype(kind)


def heavy_noise(stream_key, shape, deviation, reach, split, heavy, held_as=jnp.bfloat16):
    result = deviation * jax.random.normal(stream_key, shape, jnp.float32)
    if split:
        result = result * level_of(stream_key, shape, split, -0.22, 0.18)
    return jnp.clip(with_spikes(result, jax.random.fold_in(stream_key, 3), *heavy), -reach, reach).astype(held_as)


def setup_inputs(seed: int = 0) -> dict:
    arg_keys = jax.random.split(jax.random.key(seed), 7)
    tokens = scatter_about(arg_keys[0], (TOKENS, MODEL_WIDTH), 1.0, 6.0, ((0, 32), (1, 16)))
    token_adapter_index_keys = jax.random.split(jax.random.fold_in(arg_keys[1], 1), TOKENS // TOK_DEV)
    token_adapter_index_turns = jax.random.permutation(jax.random.fold_in(arg_keys[1], 3), TOKENS // TOK_DEV)
    token_adapter_index = jax.vmap(lambda own, number: routed_block(jax.random.fold_in(arg_keys[1], 2), own, number, TOK_DEV, ADAPTER_COUNT, 1, CAP, 2))(token_adapter_index_keys, token_adapter_index_turns).reshape((TOKENS, 1))
    adapter_table_row = jax.random.permutation(arg_keys[2], ADAPTER_COUNT).astype(jnp.int32)
    key_value_weight = heavy_noise(arg_keys[3], (MODEL_WIDTH, COLUMN_COUNT), MODEL_WIDTH ** -0.5, 0.09375, ((0, 16),), (0, 1, 16, 2.0))
    adapter_down_weight = scatter_about(arg_keys[4], (ADAPTER_COUNT, MODEL_WIDTH, 2 * ADAPTER_RANK), MODEL_WIDTH ** -0.5, 0.0625, ((0, 32), (1, 16)))
    adapter_up_weight = scatter_about(arg_keys[5], (ADAPTER_COUNT, ADAPTER_RANK, COLUMN_COUNT), ADAPTER_RANK ** -0.5, 0.75, ((0, 32),))
    return dict(tokens=tokens, token_adapter_index=token_adapter_index, adapter_table_row=adapter_table_row, key_value_weight=key_value_weight, adapter_down_weight=adapter_down_weight, adapter_up_weight=adapter_up_weight)


adapter_scale = 0.5


def reference(tokens, token_adapter_index, adapter_table_row, key_value_weight, adapter_down_weight, adapter_up_weight):
    frozen_output = jnp.dot(tokens, key_value_weight, preferred_element_type=jnp.float32)
    token_ids = token_adapter_index[:, 0].astype(jnp.int32)
    table_iota = jnp.arange(ADAPTER_COUNT, dtype=jnp.int32)
    id_match = token_ids[:, None] == table_iota[None, :]
    table_pos = jnp.sum(jnp.where(id_match, adapter_table_row[None, :], 0), axis=1).astype(jnp.int32)
    hit_table = (table_pos[:, None] == table_iota[None, :]).astype(jnp.int32)
    hit_table = hit_table.reshape(N_ADAPTER, TOK_DEV, ADAPTER_COUNT)
    running = jnp.cumsum(hit_table, axis=1) - 1
    within = jnp.sum(running * hit_table, axis=2).reshape(TOKENS).astype(jnp.int32)
    source_block = (jnp.arange(TOKENS, dtype=jnp.int32) // TOK_DEV).astype(jnp.int32)
    extent_rows = N_ADAPTER * CAP
    position_index = (table_pos * extent_rows + source_block * CAP + within).astype(jnp.int32)
    collected_rows = jnp.zeros((ADAPTER_COUNT * extent_rows, MODEL_WIDTH), tokens.dtype).at[position_index].set(tokens)
    collected_rows = collected_rows.reshape(ADAPTER_COUNT, extent_rows, MODEL_WIDTH)
    kv_width = KVH * HD

    def adapter_grouped(operands):
        rows_in, down_table, up_table = operands
        low_rank = jnp.dot(rows_in, down_table, preferred_element_type=jnp.float32).astype(tokens.dtype)
        key_delta = jnp.dot(low_rank[:, :ADAPTER_RANK], up_table[:, :kv_width], preferred_element_type=jnp.float32)
        value_delta = jnp.dot(low_rank[:, ADAPTER_RANK:], up_table[:, kv_width:], preferred_element_type=jnp.float32)
        return jnp.concatenate([key_delta, value_delta], axis=1).astype(tokens.dtype)

    adapter_update = lax.map(adapter_grouped, (collected_rows, adapter_down_weight, adapter_up_weight)).reshape(ADAPTER_COUNT * extent_rows, COLUMN_COUNT)
    projected_output = frozen_output + adapter_scale * adapter_update[position_index].astype(jnp.float32)
    return projected_output.astype(tokens.dtype)
```

```python
import jax
import jax.numpy as jnp
from jax import lax
from jax.experimental import pallas as pl
from jax.experimental.pallas import tpu as pltpu
from jax.sharding import PartitionSpec as P

adapter_scale = 0.5
MESH = pl.DeviceIdType.MESH
F32, BF16, I32 = jnp.float32, jnp.bfloat16, jnp.int32

NY, NX, NC, NZ = 4, 4, 2, 16
NA = NY * NX * NC
TOK, FEAT, COLS = 256, 512, 128
HELD, CAP, RANK2 = 4, 8, 128
MSG = HELD * CAP
GROUP = NX * NC
ROWS = GROUP * MSG
GROUPS = (2, 1, 3, 0)
OFFSETS = ((2, 0), (2, 1), (1, 0), (1, 1), (3, 0), (3, 1), (0, 1), (0, 0))


def iota(shape, dim):
    return lax.broadcasted_iota(I32, shape, dim)


def dot(a, b):
    return jnp.dot(a, b, preferred_element_type=F32)


def kernel(
    ids_ref, table_ref, tokens_hbm, kv_hbm, down_hbm, up_hbm, out_ref,
    tok, kv, down, up, sbuf, rbuf, lbuf, ret, place, zsend, zrecv, pack,
    b1, own, r1, w2, r2,
    load_sem, self_sem, tok_send, tok_recv, ret_send, ret_recv, zs_send, zs_recv, zg_send, zg_recv,
    l1_send, l1_recv, l2_send, l2_recv, up_send, up_recv,
):
    a, z = lax.axis_index("adapter"), lax.axis_index("tensor")
    y, x, c = lax.div(a, GROUP), lax.rem(lax.div(a, NC), NX), lax.rem(a, NC)

    def at(dy, dx, dc):
        return (
            lax.rem(y + dy + NY, NY) * GROUP + lax.rem(x + dx + NX, NX) * NC + lax.rem(c + dc + NC, NC)
        )

    def along_z(dz):
        return lax.rem(z + dz + NZ, NZ)

    def plane_copy(src, dst, send, recv, peer):
        return pltpu.make_async_remote_copy(
            src, dst, send, recv, device_id={"adapter": peer}, device_id_type=MESH
        )

    def z_copy(src, dst, send, recv, peer):
        return pltpu.make_async_remote_copy(
            src, dst, send, recv, device_id={"tensor": peer}, device_id_type=MESH
        )

    def wait_bytes(ref, sem):
        pltpu.make_async_copy(ref, ref, sem).wait()

    loads = [
        pltpu.make_async_copy(tokens_hbm, tok, load_sem.at[0]),
        pltpu.make_async_copy(kv_hbm, kv, load_sem.at[1]),
        pltpu.make_async_copy(down_hbm, down, load_sem.at[2]),
        pltpu.make_async_copy(
            up_hbm.at[:, :, pl.ds(pl.multiple_of(z * COLS, COLS), COLS)], up.at[y, x, c], load_sem.at[3]
        ),
    ]
    for load in loads:
        load.start()

    barrier = pltpu.get_barrier_semaphore()

    @pl.loop(1, NA)
    def _(k):
        pl.semaphore_signal(barrier, 1, device_id={"adapter": lax.rem(a + k, NA)}, device_id_type=MESH)

    @pl.loop(1, NZ)
    def _(k):
        pl.semaphore_signal(barrier, 1, device_id={"tensor": lax.rem(z + k, NZ)}, device_id_type=MESH)

    names = iota((128, TOK), 0)
    table = jnp.broadcast_to(table_ref[...].astype(F32), (8, 128)).astype(BF16)
    hit_id = (names == ids_ref[...]).astype(F32).astype(BF16)
    row = dot(table, hit_id)[0:1]
    hit = names == row.astype(I32)
    hit_f = hit.astype(F32)
    square0, square1 = iota((TOK, TOK), 0), iota((TOK, TOK), 1)
    earlier = dot(hit_f.astype(BF16), (square0 < square1).astype(F32).astype(BF16))
    within = jnp.sum(hit_f * earlier, axis=0, keepdims=True)
    slot = row.astype(I32) * CAP + within.astype(I32)

    def slots_of(r):
        return (
            lax.rem(x + lax.div(r, 2 * MSG), NX) * (NC * MSG)
            + lax.rem(c + lax.div(r, MSG), NC) * MSG
            + lax.rem(r, MSG)
        )

    loads[0].wait()
    in_row = slots_of(square0)
    token_copies = {}
    for turn, dy in enumerate(GROUPS):
        first = lax.rem(y + dy, NY) * ROWS
        chosen = (in_row == slot - first).astype(F32).astype(BF16)
        sbuf[dy * GROUP : (dy + 1) * GROUP] = dot(chosen, tok[...]).astype(BF16).reshape(GROUP, MSG, FEAT)
        if turn == 0:
            pl.semaphore_wait(barrier, NA - 1 + NZ - 1)
        for dx, dc in OFFSETS:
            k = dy * GROUP + dx * NC + dc
            if k == 0:
                token_copies[k] = pltpu.make_async_copy(sbuf.at[0], rbuf.at[0], self_sem)
            else:
                token_copies[k] = plane_copy(sbuf.at[k], rbuf.at[k], tok_send, tok_recv.at[dy], at(dy, dx, dc))
            token_copies[k].start()

    loads[1].wait()

    def part(dz, j):
        d = along_z(dz + 4 * j)
        return dot(tok[...], kv[:, pl.ds(pl.multiple_of(d * COLS, COLS), COLS)])

    half = TOK // 2
    for j in (2, 1, 3, 0):
        b1[0, j] = part(1, j).astype(BF16)
        z_copy(b1.at[0, j], r1.at[0, j], l1_send, l1_recv.at[j], along_z(1)).start()
        b1[1, j] = part(-1, j).astype(BF16)
        z_copy(b1.at[1, j], r1.at[1, j], l1_send, l1_recv.at[j], along_z(-1)).start()
        b1[2, j] = part(2, j).astype(BF16)
        i = (j + 1) % 4
        low, high = pl.ds(0, half), pl.ds(half, half)
        z_copy(b1.at[2, j, high], r1.at[2, j, high], l1_send, l1_recv.at[j], along_z(2)).start()
        z_copy(b1.at[2, j, low], r1.at[2, i, low], l1_send, l1_recv.at[i], along_z(-2)).start()

    loads[3].wait()

    def first_axis(k):
        return jnp.where(c == 0, at(0, k, 0), at(k, 0, 0))

    def second_axis(k):
        return jnp.where(c == 0, at(k, 0, 0), at(0, k, 0))

    for k in (2, 1, 3):
        plane_copy(up.at[y, x, c], up.at[y, x, c], up_send.at[0], up_recv.at[0], first_axis(k)).start()

    for j in range(4):
        own[j] = part(0, j)

    diagonal = square0 == square1
    ones = jnp.ones((TOK, 128), BF16)
    row_at = dot(jnp.where(diagonal, row, 0.0).astype(BF16), ones)
    within_at = dot(jnp.where(diagonal, within, 0.0).astype(BF16), ones)
    slot_at = (row_at * CAP + within_at).astype(I32)
    slot_at = jnp.concatenate([slot_at, slot_at], axis=1)
    in_row = slots_of(square1)
    for dy in range(NY):
        first = lax.rem(y + dy, NY) * ROWS
        place[dy] = (in_row == slot_at - first).astype(F32).astype(BF16)

    loads[2].wait()
    left = jnp.concatenate([down[0], down[1]], axis=1)
    right = jnp.concatenate([down[2], down[3]], axis=1)
    which = lax.rem(lax.div(iota((ROWS, RANK2), 0), CAP), HELD)
    for turn, j in enumerate((2, 1, 3, 0)):
        wait_bytes(r1.at[:, j], l1_recv.at[j])
        window = own[j] + r1[0, j].astype(F32) + r1[1, j].astype(F32) + r1[2, j].astype(F32)
        if j == 0:
            own[0] = window
        else:
            w2[j - 1] = window.astype(BF16)
            z_copy(w2.at[j - 1], r2.at[j - 1], l2_send, l2_recv, along_z(4 * j)).start()

        dy = GROUPS[turn]
        lo = dy * GROUP
        if dy == 0:
            wait_bytes(rbuf.at[1:GROUP], tok_recv.at[0])
            token_copies[0].wait()
        else:
            wait_bytes(rbuf.at[lo : lo + GROUP], tok_recv.at[dy])
        arrived = rbuf[lo : lo + GROUP].reshape(ROWS, FEAT)
        l01, l23 = dot(arrived, left), dot(arrived, right)
        low_rank = jnp.where(
            which < 2,
            jnp.where(which == 0, l01[:, :RANK2], l01[:, RANK2:]),
            jnp.where(which == 2, l23[:, :RANK2], l23[:, RANK2:]),
        ).astype(BF16)
        lbuf[lo : lo + GROUP] = low_rank.reshape(GROUP, MSG, RANK2)
        for dx, dc in OFFSETS:
            k = lo + dx * NC + dc
            if k == 0:
                ret[0] = lbuf[0]
            else:
                plane_copy(lbuf.at[k], ret.at[k], ret_send, ret_recv.at[dy], at(-dy, -dx, -dc)).start()

    wait_bytes(up.at[0, 0:3, 0], up_recv.at[0])

    @pl.when(c == 0)
    def _():
        for k in (2, 1, 3):
            plane_copy(up.at[y, :, 0], up.at[y, :, 0], up_send.at[1], up_recv.at[1], at(k, 0, 0)).start()

    @pl.when(c == 1)
    def _():
        for k in (2, 1, 3):
            plane_copy(up.at[:, x, 1], up.at[:, x, 1], up_send.at[1], up_recv.at[1], at(0, k, 0)).start()

    low_rank = jnp.zeros((TOK, RANK2), F32)
    for dy in GROUPS:
        lo = dy * GROUP
        wait_bytes(ret.at[max(lo, 1) : lo + GROUP], ret_recv.at[dy])
        low_rank += dot(place[dy], ret[lo : lo + GROUP].reshape(ROWS, RANK2))
    upper, lower = low_rank[:half], low_rank[half:]
    first_lanes = iota((half, RANK2), 1) < RANK2 // 2
    keys = jnp.where(first_lanes, upper, pltpu.roll(lower, RANK2 // 2, 1))
    values = jnp.where(first_lanes, pltpu.roll(upper, RANK2 // 2, 1), lower)
    zsend[0:8] = keys.astype(BF16).reshape(8, 16, RANK2)
    zsend[8:16] = values.astype(BF16).reshape(8, 16, RANK2)
    for k in (8, 7, 9, 6, 10, 5, 11, 4, 12, 3, 13, 2, 14, 1, 15):
        z_copy(zsend.at[along_z(k)], zrecv.at[k - 1], zs_send, zs_recv, along_z(k)).start()

    wait_bytes(r2, l2_recv)
    own[0] = own[0] + r2[0].astype(F32) + r2[1].astype(F32) + r2[2].astype(F32)

    wait_bytes(up.at[0:3, :, 0], up_recv.at[1])
    other = at(0, 0, 1)
    plane_copy(up.at[:, :, c], up.at[:, :, c], up_send.at[2], up_recv.at[2], other).start()

    wait_bytes(zrecv, zs_recv)
    total = zsend[z].astype(F32)
    for k in range(NZ - 1):
        total += zrecv[k].astype(F32)
    spot, side = lax.rem(z, 8), lax.div(z, 8) * 8
    pack[spot] = total.astype(BF16)
    for k in (4, 3, 5, 2, 6, 1, 7):
        z_copy(pack.at[spot], pack.at[spot], zg_send, zg_recv, side + lax.rem(spot + k, 8)).start()

    wait_bytes(up.at[:, :, 0], up_recv.at[2])
    wait_bytes(pack.at[0:7], zg_recv)

    full = pack[...].reshape(half, RANK2).astype(F32)
    turned = pltpu.roll(full, RANK2 // 2, 1)
    twice = jnp.concatenate(
        [jnp.where(first_lanes, full, turned), jnp.where(first_lanes, turned, full)], axis=0
    ).astype(BF16)
    twice = jnp.concatenate([twice, twice], axis=1)
    lane = lax.div(iota((TOK, 256), 1), RANK2 // 2)
    shifted = jnp.concatenate([row_at, row_at], axis=1).astype(I32) - lane
    delta = jnp.zeros((TOK, COLS), F32)
    for h in range(NA):
        block = jnp.where(shifted == HELD * h, twice, jnp.zeros_like(twice))
        delta += dot(block, up[h // GROUP, h // NC % NX, h % NC].reshape(HELD * 64, COLS))
    result = own[0] + adapter_scale * delta.astype(BF16).astype(F32)
    out_ref[...] = result.astype(BF16)

    wait_bytes(sbuf.at[1:NA], tok_send)
    wait_bytes(lbuf.at[1:NA], ret_send)
    wait_bytes(b1, l1_send)
    wait_bytes(w2, l2_send)
    wait_bytes(zrecv, zs_send)
    wait_bytes(pack.at[0:7], zg_send)
    wait_bytes(up.at[0, 0:3, 0], up_send.at[0])
    wait_bytes(up.at[0:3, :, 0], up_send.at[1])
    wait_bytes(up.at[:, :, 0], up_send.at[2])


def per_device(tokens, token_adapter_index, adapter_table_row, kv_weight, down_weight, up_weight):
    dma = pltpu.SemaphoreType.DMA
    vmem = pltpu.VMEM
    call = pl.pallas_call(
        kernel,
        out_shape=jax.ShapeDtypeStruct((TOK, COLS), BF16),
        in_specs=[pl.BlockSpec(memory_space=pltpu.VMEM)] * 2 + [pl.BlockSpec(memory_space=pl.ANY)] * 4,
        out_specs=pl.BlockSpec(memory_space=pltpu.VMEM),
        scratch_shapes=[
            vmem((TOK, FEAT), BF16),
            vmem((FEAT, NZ * COLS), BF16),
            vmem((HELD, FEAT, RANK2), BF16),
            vmem((NY, NX, NC, HELD, RANK2 // 2, COLS), BF16),
            vmem((NA, MSG, FEAT), BF16),
            vmem((NA, MSG, FEAT), BF16),
            vmem((NA, MSG, RANK2), BF16),
            vmem((NA, MSG, RANK2), BF16),
            vmem((NY, TOK, ROWS), BF16),
            vmem((NZ, 16, RANK2), BF16),
            vmem((NZ - 1, 16, RANK2), BF16),
            vmem((8, 16, RANK2), BF16),
            vmem((3, 4, TOK, COLS), BF16),
            vmem((4, TOK, COLS), F32),
            vmem((3, 4, TOK, COLS), BF16),
            vmem((3, TOK, COLS), BF16),
            vmem((3, TOK, COLS), BF16),
            dma((4,)),
            dma,
            dma,
            dma((NY,)),
            dma,
            dma((NY,)),
            dma,
            dma,
            dma,
            dma,
            dma,
            dma((4,)),
            dma,
            dma,
            dma((3,)),
            dma((3,)),
        ],
        compiler_params=pltpu.CompilerParams(
            collective_id=0, has_side_effects=True, vmem_limit_bytes=40 << 20
        ),
        name="lora_kv",
    )
    return call(
        token_adapter_index.reshape(1, TOK),
        adapter_table_row.reshape(1, 128),
        tokens,
        kv_weight,
        down_weight,
        up_weight,
    )


def solution(mesh):
    return jax.shard_map(
        per_device,
        mesh=mesh,
        in_specs=(
            P("adapter", "tensor"),
            P("adapter", None),
            P(),
            P("tensor", None),
            P("adapter", "tensor", None),
            P("adapter", None, None),
        ),
        out_specs=P("adapter", "tensor"),
        check_vma=False,
    )
```

```python
import jax
import jax.numpy as jnp
from jax import lax
from jax.experimental import pallas as pl
from jax.experimental.pallas import tpu as pltpu
from jax.sharding import PartitionSpec as P

CENTRES = (6, -6, 3, -3, 0)
LEAVES = ((0, 2), (0, 1), (0, -1), (1, 1), (1, -1), (2, 1), (2, -1), (3, 1), (3, -1), (4, 1), (4, -1))
WINDOWS = ((0, 1), (2,), (3,), (4,))

adapter_scale = 0.5
MESH = pl.DeviceIdType.MESH
F32, BF16, I32 = jnp.float32, jnp.bfloat16, jnp.int32

NY, NX, NC, NZ = 4, 4, 2, 16
NA = NY * NX * NC
TOK, FEAT, COLS = 256, 512, 128
HELD, CAP, RANK2 = 4, 8, 128
MSG = HELD * CAP
GROUP = NX * NC
ROWS = GROUP * MSG
GROUPS = (2, 1, 3, 0)
OFFSETS = ((2, 0), (2, 1), (1, 0), (1, 1), (3, 0), (3, 1), (0, 1), (0, 0))


def iota(shape, dim):
    return lax.broadcasted_iota(I32, shape, dim)


def dot(a, b):
    return jnp.dot(a, b, preferred_element_type=F32)


def kernel(
    ids_hbm, table_hbm, tokens_hbm, kv_hbm, down_hbm, up_hbm, out_ref,
    ids, names_row, tok, kv, down, up, sbuf, rbuf, lbuf, ret, place, zsend, zrecv, pack,
    b1, own, r1, w2, r2,
    load_sem, self_sem, tok_send, tok_recv, ret_send, ret_recv, zs_send, zs_recv, zg_send, zg_recv,
    l1_send, l1_recv, l2_send, l2_recv, up_send, up_recv, far_sem, farther_sem,
):
    a, z = lax.axis_index("adapter"), lax.axis_index("tensor")
    y, x, c = lax.div(a, GROUP), lax.rem(lax.div(a, NC), NX), lax.rem(a, NC)
    pend = {}

    def at(dy, dx, dc):
        return (
            lax.rem(y + dy + NY, NY) * GROUP + lax.rem(x + dx + NX, NX) * NC + lax.rem(c + dc + NC, NC)
        )

    def along_z(dz):
        return lax.rem(z + dz + NZ, NZ)

    def plane_copy(src, dst, send, recv, peer):
        return pltpu.make_async_remote_copy(
            src, dst, send, recv, device_id={"adapter": peer}, device_id_type=MESH
        )

    def z_copy(src, dst, send, recv, peer):
        return pltpu.make_async_remote_copy(
            src, dst, send, recv, device_id={"tensor": peer}, device_id_type=MESH
        )

    def wait_bytes(ref, sem):
        pltpu.make_async_copy(ref, ref, sem).wait()

    def later(name, ref, sem):
        pend[name] = (ref, sem)

    def due(name):
        wait_bytes(*pend.pop(name))

    def signal_z(sem, dz):
        pl.semaphore_signal(sem, 1, device_id={"tensor": along_z(dz)}, device_id_type=MESH)

    loads = [
        pltpu.make_async_copy(ids_hbm, ids, load_sem.at[4]),
        pltpu.make_async_copy(table_hbm, names_row, load_sem.at[5]),
        pltpu.make_async_copy(tokens_hbm, tok, load_sem.at[0]),
        pltpu.make_async_copy(kv_hbm, kv, load_sem.at[1]),
        pltpu.make_async_copy(down_hbm, down, load_sem.at[2]),
        pltpu.make_async_copy(
            up_hbm.at[:, :, pl.ds(pl.multiple_of(z * COLS, COLS), COLS)], up.at[y, x, c], load_sem.at[3]
        ),
    ]
    for load in loads:
        load.start()

    barrier = pltpu.get_barrier_semaphore()

    @pl.loop(1, NA)
    def _(k):
        pl.semaphore_signal(barrier, 1, device_id={"adapter": lax.rem(a + k, NA)}, device_id_type=MESH)

    for dz in (1, -1, 2, -2):
        signal_z(barrier, dz)

    names = iota((128, TOK), 0)
    loads[0].wait()
    loads[1].wait()
    table = jnp.broadcast_to(names_row[...].astype(F32), (8, 128)).astype(BF16)
    hit_id = (names == ids[...]).astype(F32).astype(BF16)
    row = dot(table, hit_id)[0:1]
    hit = names == row.astype(I32)
    hit_f = hit.astype(F32)
    square0, square1 = iota((TOK, TOK), 0), iota((TOK, TOK), 1)
    earlier = dot(hit_f.astype(BF16), (square0 < square1).astype(F32).astype(BF16))
    within = jnp.sum(hit_f * earlier, axis=0, keepdims=True)
    slot = row.astype(I32) * CAP + within.astype(I32)

    def slots_of(r):
        return (((x + (r >> 6)) & (NX - 1)) << 6) | (((c + (r >> 5)) & (NC - 1)) << 5) | (r & (MSG - 1))

    def part(dz):
        d = along_z(dz)
        return dot(tok[...], kv[:, pl.ds(pl.multiple_of(d * COLS, COLS), COLS)])

    loads[2].wait()
    in_row = slots_of(square0)
    half = TOK // 2
    for turn, dy in enumerate(GROUPS):
        first = lax.rem(y + dy, NY) * ROWS
        chosen = (in_row == slot - first).astype(F32).astype(BF16)
        sbuf[dy * GROUP : (dy + 1) * GROUP] = dot(chosen, tok[...]).astype(BF16).reshape(GROUP, MSG, FEAT)
        if turn == 0:
            pl.semaphore_wait(barrier, NA - 1 + 4)
            signal_z(far_sem, 2)
            signal_z(far_sem, -2)
        for dx, dc in OFFSETS:
            k = dy * GROUP + dx * NC + dc
            if k == 0:
                copy = pltpu.make_async_copy(sbuf.at[0], rbuf.at[0], self_sem)
                later("self", sbuf.at[0], self_sem)
            else:
                copy = plane_copy(sbuf.at[k], rbuf.at[k], tok_send, tok_recv.at[dy], at(dy, dx, dc))
            copy.start()
        lo = dy * GROUP
        later(f"tok{dy}", rbuf.at[max(lo, 1) : lo + GROUP], tok_recv.at[dy])
        if turn == 0:
            loads[3].wait()
        for w in WINDOWS[turn]:
            for dz in (2, 1, -1) if w == 0 else (1, -1):
                k = LEAVES.index((w, dz))
                b1[k] = part(dz + CENTRES[w]).astype(BF16)
                z_copy(b1.at[k], r1.at[k], l1_send, l1_recv.at[w], along_z(dz)).start()
            k = LEAVES.index((w, 1))
            later(f"l1{w}", r1.at[0:3] if w == 0 else r1.at[k : k + 2], l1_recv.at[w])
    later("tok_send", sbuf.at[1:NA], tok_send)
    later("l1_send", b1, l1_send)
    for w in range(5):
        own[w] = part(CENTRES[w])
    pl.semaphore_wait(far_sem, 2)
    signal_z(farther_sem, 4)
    signal_z(farther_sem, -4)

    loads[5].wait()

    def first_axis(k):
        return jnp.where(c == 0, at(0, k, 0), at(k, 0, 0))

    for k in (2, 1, 3):
        plane_copy(up.at[y, x, c], up.at[y, x, c], up_send.at[0], up_recv.at[0], first_axis(k)).start()
    later("up0", up.at[0, 0:3, 0], up_recv.at[0])
    later("up_send0", up.at[0, 0:3, 0], up_send.at[0])

    diagonal = square0 == square1
    ones = jnp.ones((TOK, 128), BF16)
    row_at = dot(jnp.where(diagonal, row, 0.0).astype(BF16), ones)
    within_at = dot(jnp.where(diagonal, within, 0.0).astype(BF16), ones)
    slot_at = (row_at * CAP + within_at).astype(I32)
    slot_at = jnp.concatenate([slot_at, slot_at], axis=1)
    in_row = slots_of(square1)
    for dy in range(NY):
        first = lax.rem(y + dy, NY) * ROWS
        place[dy] = (in_row == slot_at - first).astype(F32).astype(BF16)

    loads[4].wait()
    left = jnp.concatenate([down[0], down[1]], axis=1)
    right = jnp.concatenate([down[2], down[3]], axis=1)
    which = (iota((ROWS, RANK2), 0) >> 3) & (HELD - 1)
    def window(w):
        due(f"l1{w}")
        k = LEAVES.index((w, 1))
        total = own[w] + r1[k].astype(F32) + r1[k + 1].astype(F32)
        return total + r1[0].astype(F32) if w == 0 else total

    def outer(w):
        w2[w] = window(w).astype(BF16)
        z_copy(w2.at[w], r2.at[w], l2_send, l2_recv.at[w], along_z(CENTRES[w] // 2)).start()
        later(f"l2{w}", r2.at[w], l2_recv.at[w])

    def inner(w):
        due(f"l2{w - 2}")
        w2[w] = (window(w) + r2[w - 2].astype(F32)).astype(BF16)
        z_copy(w2.at[w], r2.at[w], l2_send, l2_recv.at[w], along_z(CENTRES[w])).start()
        later(f"l2{w}", r2.at[w], l2_recv.at[w])

    def root():
        total = window(4)
        due("l22")
        due("l23")
        own[4] = total + r2[2].astype(F32) + r2[3].astype(F32)

    def token_step(dy):
        lo = dy * GROUP
        due(f"tok{dy}")
        if dy == 0:
            due("self")
        arrived = rbuf[lo : lo + GROUP].reshape(ROWS, FEAT)
        l01, l23 = dot(arrived, left), dot(arrived, right)
        low_rank = jnp.where(
            which < 2,
            jnp.where(which == 0, l01[:, :RANK2], l01[:, RANK2:]),
            jnp.where(which == 2, l23[:, :RANK2], l23[:, RANK2:]),
        ).astype(BF16)
        lbuf[lo : lo + GROUP] = low_rank.reshape(GROUP, MSG, RANK2)
        for dx, dc in OFFSETS:
            k = lo + dx * NC + dc
            if k == 0:
                ret[0] = lbuf[0]
            else:
                plane_copy(lbuf.at[k], ret.at[k], ret_send, ret_recv.at[dy], at(-dy, -dx, -dc)).start()
        later(f"ret{dy}", ret.at[max(lo, 1) : lo + GROUP], ret_recv.at[dy])
    outer(0)
    outer(1)
    token_step(2)
    token_step(1)
    inner(2)
    inner(3)
    token_step(3)
    token_step(0)
    later("l2_send", w2, l2_send)
    later("ret_send", lbuf.at[1:NA], ret_send)

    due("up0")

    @pl.when(c == 0)
    def _():
        for k in (2, 1, 3):
            plane_copy(up.at[y, :, 0], up.at[y, :, 0], up_send.at[1], up_recv.at[1], at(k, 0, 0)).start()

    @pl.when(c == 1)
    def _():
        for k in (2, 1, 3):
            plane_copy(up.at[:, x, 1], up.at[:, x, 1], up_send.at[1], up_recv.at[1], at(0, k, 0)).start()
    later("up1", up.at[0:3, :, 0], up_recv.at[1])
    later("up_send1", up.at[0:3, :, 0], up_send.at[1])

    low_rank = jnp.zeros((TOK, RANK2), F32)
    for dy in GROUPS:
        lo = dy * GROUP
        due(f"ret{dy}")
        low_rank += dot(place[dy], ret[lo : lo + GROUP].reshape(ROWS, RANK2))
    upper, lower = low_rank[:half], low_rank[half:]
    first_lanes = iota((half, RANK2), 1) < RANK2 // 2
    keys = jnp.where(first_lanes, upper, pltpu.roll(lower, RANK2 // 2, 1))
    values = jnp.where(first_lanes, pltpu.roll(upper, RANK2 // 2, 1), lower)
    zsend[0:8] = keys.astype(BF16).reshape(8, 16, RANK2)
    zsend[8:16] = values.astype(BF16).reshape(8, 16, RANK2)
    pl.semaphore_wait(farther_sem, 2)
    for k in (8, 7, 9, 6, 10, 5, 11, 4, 12, 3, 13, 2, 14, 1, 15):
        z_copy(zsend.at[along_z(k)], zrecv.at[k - 1], zs_send, zs_recv, along_z(k)).start()
    later("zs", zrecv, zs_recv)
    later("zs_send", zrecv, zs_send)

    due("zs")
    total = zsend[z].astype(F32)
    for k in range(NZ - 1):
        total += zrecv[k].astype(F32)
    spot, side = lax.rem(z, 8), lax.div(z, 8) * 8
    pack[spot] = total.astype(BF16)
    for k in (4, 3, 5, 2, 6, 1, 7):
        z_copy(pack.at[spot], pack.at[spot], zg_send, zg_recv, side + lax.rem(spot + k, 8)).start()
    later("zg", pack.at[0:7], zg_recv)
    later("zg_send", pack.at[0:7], zg_send)

    due("up1")
    other = at(0, 0, 1)
    plane_copy(up.at[:, :, c], up.at[:, :, c], up_send.at[2], up_recv.at[2], other).start()
    later("up2", up.at[:, :, 0], up_recv.at[2])
    later("up_send2", up.at[:, :, 0], up_send.at[2])

    root()

    due("zg")
    due("up2")

    full = pack[...].reshape(half, RANK2).astype(F32)
    turned = pltpu.roll(full, RANK2 // 2, 1)
    twice = jnp.concatenate(
        [jnp.where(first_lanes, full, turned), jnp.where(first_lanes, turned, full)], axis=0
    ).astype(BF16)
    twice = jnp.concatenate([twice, twice], axis=1)
    lane = iota((TOK, 256), 1) >> 6
    shifted = jnp.concatenate([row_at, row_at], axis=1).astype(I32) - lane
    delta = jnp.zeros((TOK, COLS), F32)
    for h in range(NA):
        block = jnp.where(shifted == HELD * h, twice, jnp.zeros_like(twice))
        delta += dot(block, up[h // GROUP, h // NC % NX, h % NC].reshape(HELD * 64, COLS))
    result = own[4] + adapter_scale * delta
    out_ref[...] = result.astype(BF16)
    for n in list(pend):
        due(n)


def per_device(tokens, token_adapter_index, adapter_table_row, kv_weight, down_weight, up_weight):
    dma = pltpu.SemaphoreType.DMA
    vmem = pltpu.VMEM
    call = pl.pallas_call(
        kernel,
        out_shape=jax.ShapeDtypeStruct((TOK, COLS), BF16),
        in_specs=[pl.BlockSpec(memory_space=pl.ANY)] * 6,
        out_specs=pl.BlockSpec(memory_space=pltpu.VMEM),
        scratch_shapes=[
            vmem((1, TOK), I32),
            vmem((1, 128), I32),
            vmem((TOK, FEAT), BF16),
            vmem((FEAT, NZ * COLS), BF16),
            vmem((HELD, FEAT, RANK2), BF16),
            vmem((NY, NX, NC, HELD, RANK2 // 2, COLS), BF16),
            vmem((NA, MSG, FEAT), BF16),
            vmem((NA, MSG, FEAT), BF16),
            vmem((NA, MSG, RANK2), BF16),
            vmem((NA, MSG, RANK2), BF16),
            vmem((NY, TOK, ROWS), BF16),
            vmem((NZ, 16, RANK2), BF16),
            vmem((NZ - 1, 16, RANK2), BF16),
            vmem((8, 16, RANK2), BF16),
            vmem((len(LEAVES), TOK, COLS), BF16),
            vmem((5, TOK, COLS), F32),
            vmem((len(LEAVES), TOK, COLS), BF16),
            vmem((4, TOK, COLS), BF16),
            vmem((4, TOK, COLS), BF16),
            dma((6,)),
            dma,
            dma,
            dma((NY,)),
            dma,
            dma((NY,)),
            dma,
            dma,
            dma,
            dma,
            dma,
            dma((5,)),
            dma,
            dma((4,)),
            dma((3,)),
            dma((3,)),
            pltpu.SemaphoreType.REGULAR,
            pltpu.SemaphoreType.REGULAR,
        ],
        compiler_params=pltpu.CompilerParams(
            collective_id=0, has_side_effects=True, vmem_limit_bytes=60 << 20
        ),
        name="lora_kv",
    )
    return call(
        token_adapter_index.reshape(1, TOK),
        adapter_table_row.reshape(1, 128),
        tokens,
        kv_weight,
        down_weight,
        up_weight,
    )


def solution(mesh):
    return jax.shard_map(
        per_device,
        mesh=mesh,
        in_specs=(
            P("adapter", "tensor"),
            P("adapter", None),
            P(),
            P("tensor", None),
            P("adapter", "tensor", None),
            P("adapter", None, None),
        ),
        out_specs=P("adapter", "tensor"),
        check_vma=False,
    )
```

```python
import jax
import jax.numpy as jnp
from jax import lax
from jax.experimental import pallas as pl
from jax.experimental.pallas import tpu as pltpu
from jax.sharding import PartitionSpec as P

CENTRES = (6, -6, 3, -3, 0)
LEAVES = ((0, 2), (0, 1), (0, -1), (1, 1), (1, -1), (2, 1), (2, -1), (3, 1), (3, -1), (4, 1), (4, -1))
WINDOWS = ((0, 1), (2,), (3,), (4,))

adapter_scale = 0.5
MESH = pl.DeviceIdType.MESH
F32, BF16, I32 = jnp.float32, jnp.bfloat16, jnp.int32

NY, NX, NC, NZ = 4, 4, 2, 16
NA = NY * NX * NC
TOK, FEAT, COLS = 256, 512, 128
HELD, CAP, RANK2 = 4, 8, 128
MSG = HELD * CAP
GROUP = NX * NC
ROWS = GROUP * MSG
GROUPS = (0, 1, 3, 2)
MEMBERS = {
    s: [(dy, (s - dy) % NX, dc, dy * NC + dc) for dy in (2, 1, 3, 0) for dc in (0, 1)] for s in GROUPS
}


def iota(shape, dim):
    return lax.broadcasted_iota(I32, shape, dim)


def dot(a, b):
    return jnp.dot(a, b, preferred_element_type=F32)


def kernel(
    ids_hbm, table_hbm, tokens_hbm, kv_hbm, down_hbm, up_hbm, out_ref,
    ids, names_row, tok, kv, down, up, sbuf, rbuf, lbuf, ret, place, zsend, zrecv, zown, pack,
    b1, own, r1, w2, r2,
    load_sem, self_sem, tok_send, tok_recv, ret_send, ret_recv, zs_send, zs_recv, zg_send, zg_recv,
    l1_send, l1_recv, l2_send, l2_recv, up_send, up_recv, far_sem, farther_sem,
):
    a, z = lax.axis_index("adapter"), lax.axis_index("tensor")
    y, x, c = lax.div(a, GROUP), lax.rem(lax.div(a, NC), NX), lax.rem(a, NC)
    pend = {}

    def at(dy, dx, dc):
        return (
            lax.rem(y + dy + NY, NY) * GROUP + lax.rem(x + dx + NX, NX) * NC + lax.rem(c + dc + NC, NC)
        )

    def along_z(dz):
        return lax.rem(z + dz + NZ, NZ)

    def plane_copy(src, dst, send, recv, peer):
        return pltpu.make_async_remote_copy(
            src, dst, send, recv, device_id={"adapter": peer}, device_id_type=MESH
        )

    def z_copy(src, dst, send, recv, peer):
        return pltpu.make_async_remote_copy(
            src, dst, send, recv, device_id={"tensor": peer}, device_id_type=MESH
        )

    def wait_bytes(ref, sem):
        pltpu.make_async_copy(ref, ref, sem).wait()

    def later(name, ref, sem):
        pend[name] = (ref, sem)

    def due(name):
        wait_bytes(*pend.pop(name))

    def signal_z(sem, dz):
        pl.semaphore_signal(sem, 1, device_id={"tensor": along_z(dz)}, device_id_type=MESH)

    loads = [
        pltpu.make_async_copy(ids_hbm, ids, load_sem.at[4]),
        pltpu.make_async_copy(table_hbm, names_row, load_sem.at[5]),
        pltpu.make_async_copy(tokens_hbm, tok, load_sem.at[0]),
        pltpu.make_async_copy(kv_hbm, kv, load_sem.at[1]),
        pltpu.make_async_copy(down_hbm, down, load_sem.at[2]),
        pltpu.make_async_copy(
            up_hbm.at[:, :, pl.ds(pl.multiple_of(z * COLS, COLS), COLS)], up.at[y, x, c], load_sem.at[3]
        ),
    ]
    for load in loads:
        load.start()

    barrier = pltpu.get_barrier_semaphore()

    @pl.loop(1, NA)
    def _(k):
        pl.semaphore_signal(barrier, 1, device_id={"adapter": lax.rem(a + k, NA)}, device_id_type=MESH)

    for dz in (1, -1, 2, -2):
        signal_z(barrier, dz)

    names = iota((128, TOK), 0)
    loads[0].wait()
    loads[1].wait()
    table = jnp.broadcast_to(names_row[...].astype(F32), (8, 128)).astype(BF16)
    hit_id = (names == ids[...]).astype(F32).astype(BF16)
    row = dot(table, hit_id)[0:1]
    hit = names == row.astype(I32)
    hit_f = hit.astype(F32)
    square0, square1 = iota((TOK, TOK), 0), iota((TOK, TOK), 1)
    earlier = dot(hit_f.astype(BF16), (square0 < square1).astype(F32).astype(BF16))
    within = jnp.sum(hit_f * earlier, axis=0, keepdims=True)
    slot = row.astype(I32) * CAP + within.astype(I32)

    def slots_of(r, s):
        dy = r >> 6
        row_first = ((y + dy) & (NY - 1)) << 8
        chip_first = ((x + s + NX - dy) & (NX - 1)) << 6
        return row_first | chip_first | (((c + (r >> 5)) & (NC - 1)) << 5) | (r & (MSG - 1))

    def part(dz):
        d = along_z(dz)
        return dot(tok[...], kv[:, pl.ds(pl.multiple_of(d * COLS, COLS), COLS)])

    loads[2].wait()
    half = TOK // 2
    for turn, dy in enumerate(GROUPS):
        chosen = (slots_of(square0, dy) == slot).astype(F32).astype(BF16)
        sbuf[dy * GROUP : (dy + 1) * GROUP] = dot(chosen, tok[...]).astype(BF16).reshape(GROUP, MSG, FEAT)
        if turn == 0:
            pl.semaphore_wait(barrier, NA - 1 + 4)
            signal_z(far_sem, 2)
            signal_z(far_sem, -2)
        for my, mx, mc, i in MEMBERS[dy]:
            k = dy * GROUP + i
            if k == 0:
                copy = pltpu.make_async_copy(sbuf.at[0], rbuf.at[0], self_sem)
                later("self", sbuf.at[0], self_sem)
            else:
                copy = plane_copy(sbuf.at[k], rbuf.at[k], tok_send, tok_recv.at[dy], at(my, mx, mc))
            copy.start()
        lo = dy * GROUP
        later(f"tok{dy}", rbuf.at[max(lo, 1) : lo + GROUP], tok_recv.at[dy])
        if turn == 0:
            loads[3].wait()
        for w in WINDOWS[turn]:
            for dz in (2, 1, -1) if w == 0 else (1, -1):
                k = LEAVES.index((w, dz))
                b1[k] = part(dz + CENTRES[w]).astype(BF16)
                z_copy(b1.at[k], r1.at[k], l1_send, l1_recv.at[w], along_z(dz)).start()
            k = LEAVES.index((w, 1))
            later(f"l1{w}", r1.at[0:3] if w == 0 else r1.at[k : k + 2], l1_recv.at[w])
    later("tok_send", sbuf.at[1:NA], tok_send)
    later("l1_send", b1, l1_send)
    for w in range(5):
        own[w] = part(CENTRES[w])
    pl.semaphore_wait(far_sem, 2)
    signal_z(farther_sem, 4)
    signal_z(farther_sem, -4)

    loads[5].wait()

    def first_axis(k):
        return jnp.where(c == 0, at(0, k, 0), at(k, 0, 0))

    diagonal = square0 == square1
    ones = jnp.ones((TOK, 128), BF16)
    row_at = dot(jnp.where(diagonal, row, 0.0).astype(BF16), ones)
    within_at = dot(jnp.where(diagonal, within, 0.0).astype(BF16), ones)
    slot_at = (row_at * CAP + within_at).astype(I32)
    slot_at = jnp.concatenate([slot_at, slot_at], axis=1)
    for dy in GROUPS:
        place[dy] = (slots_of(square1, dy) == slot_at).astype(F32).astype(BF16)

    loads[4].wait()
    left = jnp.concatenate([down[0], down[1]], axis=1)
    right = jnp.concatenate([down[2], down[3]], axis=1)
    which = (iota((ROWS, RANK2), 0) >> 3) & (HELD - 1)
    def window(w):
        due(f"l1{w}")
        k = LEAVES.index((w, 1))
        total = own[w] + r1[k].astype(F32) + r1[k + 1].astype(F32)
        return total + r1[0].astype(F32) if w == 0 else total

    def encode(w, total):
        most = jnp.max(jnp.max(jnp.abs(total), axis=0, keepdims=True), axis=1, keepdims=True)
        power = jnp.ceil(jnp.log2(jnp.maximum(most, 1e-30)) + 0.01)
        w2[w, 0:TOK] = jnp.round(total * (32000.0 * jnp.exp2(-power))).astype(I32).astype(jnp.int16)
        w2[w, TOK : TOK + 16] = jnp.broadcast_to(power, (16, COLS)).astype(I32).astype(jnp.int16)

    def decode(w):
        power = r2[w, TOK : TOK + 16].astype(I32).astype(F32)[0:1]
        return r2[w, 0:TOK].astype(I32).astype(F32) * (jnp.exp2(power) * (1 / 32000.0))

    def outer(w):
        encode(w, window(w))
        z_copy(w2.at[w], r2.at[w], l2_send, l2_recv.at[w], along_z(CENTRES[w] // 2)).start()
        later(f"l2{w}", r2.at[w], l2_recv.at[w])

    def inner(w):
        due(f"l2{w - 2}")
        encode(w, window(w) + decode(w - 2))
        z_copy(w2.at[w], r2.at[w], l2_send, l2_recv.at[w], along_z(CENTRES[w])).start()
        later(f"l2{w}", r2.at[w], l2_recv.at[w])

    def root():
        total = window(4)
        due("l22")
        due("l23")
        own[4] = total + decode(2) + decode(3)

    def token_step(dy):
        lo = dy * GROUP
        due(f"tok{dy}")
        if dy == 0:
            due("self")
        arrived = rbuf[lo : lo + GROUP].reshape(ROWS, FEAT)
        l01, l23 = dot(arrived, left), dot(arrived, right)
        low_rank = jnp.where(
            which < 2,
            jnp.where(which == 0, l01[:, :RANK2], l01[:, RANK2:]),
            jnp.where(which == 2, l23[:, :RANK2], l23[:, RANK2:]),
        ).astype(BF16)
        lbuf[lo : lo + GROUP] = low_rank.reshape(GROUP, MSG, RANK2)
        for my, mx, mc, i in MEMBERS[dy]:
            k = lo + i
            if k == 0:
                ret[0] = lbuf[0]
            else:
                plane_copy(lbuf.at[k], ret.at[k], ret_send, ret_recv.at[dy], at(-my, -mx, -mc)).start()
        later(f"ret{dy}", ret.at[max(lo, 1) : lo + GROUP], ret_recv.at[dy])
    token_step(GROUPS[0])
    outer(0)
    outer(1)
    token_step(GROUPS[1])
    token_step(GROUPS[2])
    token_step(GROUPS[3])
    inner(2)
    inner(3)
    later("l2_send", w2, l2_send)
    later("ret_send", lbuf.at[1:NA], ret_send)

    for k in (2, 1, 3):
        plane_copy(up.at[y, x, c], up.at[y, x, c], up_send.at[0], up_recv.at[0], first_axis(k)).start()
    later("up0", up.at[0, 0:3, 0], up_recv.at[0])
    later("up_send0", up.at[0, 0:3, 0], up_send.at[0])

    low_rank = jnp.zeros((TOK, RANK2), F32)
    for dy in GROUPS:
        lo = dy * GROUP
        due(f"ret{dy}")
        low_rank += dot(place[dy], ret[lo : lo + GROUP].reshape(ROWS, RANK2))
    upper, lower = low_rank[:half], low_rank[half:]
    first_lanes = iota((half, RANK2), 1) < RANK2 // 2
    keys = jnp.where(first_lanes, upper, pltpu.roll(lower, RANK2 // 2, 1))
    values = jnp.where(first_lanes, pltpu.roll(upper, RANK2 // 2, 1), lower)
    zsend[0:8] = keys.astype(BF16).reshape(8, 16, RANK2)
    zsend[8:16] = values.astype(BF16).reshape(8, 16, RANK2)
    pl.semaphore_wait(farther_sem, 2)
    for k in (8, 7, 9, 6, 10, 5, 11, 4, 12, 3, 13, 2, 14, 1, 15):
        z_copy(zsend.at[along_z(k + 4 - NZ)], zrecv.at[k - 1], zs_send, zs_recv, along_z(k)).start()
    later("zs", zrecv, zs_recv)
    later("zs_send", zrecv, zs_send)

    due("up0")

    @pl.when(c == 0)
    def _():
        for k in (2, 1, 3):
            plane_copy(up.at[y, :, 0], up.at[y, :, 0], up_send.at[1], up_recv.at[1], at(k, 0, 0)).start()

    @pl.when(c == 1)
    def _():
        for k in (2, 1, 3):
            plane_copy(up.at[:, x, 1], up.at[:, x, 1], up_send.at[1], up_recv.at[1], at(0, k, 0)).start()
    later("up1", up.at[0:3, :, 0], up_recv.at[1])
    later("up_send1", up.at[0:3, :, 0], up_send.at[1])

    due("zs")
    mine = along_z(4)
    total = zsend[mine].astype(F32)
    for k in range(NZ - 1):
        total += zrecv[k].astype(F32)
    spot, side, spot_z = lax.rem(mine, 8), lax.div(mine, 8) * 8, lax.rem(z, 8)
    zown[...] = total.astype(BF16)

    @pl.when(spot >= 4)
    def _():
        pack[spot] = zown[...]

    for t in (7, 6, 5, 4, 0, 1, 2, 3):

        @pl.when(spot != t + 4)
        def _(t=t):
            z_copy(zown, pack.at[spot], zg_send, zg_recv, side + t).start()

    due("up1")
    other = at(0, 0, 1)
    plane_copy(up.at[:, :, c], up.at[:, :, c], up_send.at[2], up_recv.at[2], other).start()
    later("up2", up.at[:, :, 0], up_recv.at[2])
    later("up_send2", up.at[:, :, 0], up_send.at[2])

    root()

    @pl.when(spot_z < 4)
    def _():
        wait_bytes(pack.at[0:7], zg_recv)

    @pl.when(spot_z >= 4)
    def _():
        wait_bytes(pack, zg_recv)

    due("up2")

    full = pack[...].reshape(half, RANK2).astype(F32)
    turned = pltpu.roll(full, RANK2 // 2, 1)
    twice = jnp.concatenate(
        [jnp.where(first_lanes, full, turned), jnp.where(first_lanes, turned, full)], axis=0
    ).astype(BF16)
    twice = jnp.concatenate([twice, twice], axis=1)
    lane = iota((TOK, 256), 1) >> 6
    shifted = jnp.concatenate([row_at, row_at], axis=1).astype(I32) - lane
    delta = jnp.zeros((TOK, COLS), F32)
    for h in range(NA):
        block = jnp.where(shifted == HELD * h, twice, jnp.zeros_like(twice))
        delta += dot(block, up[h // GROUP, h // NC % NX, h % NC].reshape(HELD * 64, COLS))
    result = own[4] + adapter_scale * delta
    out_ref[...] = result.astype(BF16)

    @pl.when(spot < 4)
    def _():
        wait_bytes(pack, zg_send)

    @pl.when(spot >= 4)
    def _():
        wait_bytes(pack.at[0:7], zg_send)

    for n in list(pend):
        due(n)


def per_device(tokens, token_adapter_index, adapter_table_row, kv_weight, down_weight, up_weight):
    dma = pltpu.SemaphoreType.DMA
    vmem = pltpu.VMEM
    call = pl.pallas_call(
        kernel,
        out_shape=jax.ShapeDtypeStruct((TOK, COLS), BF16),
        in_specs=[pl.BlockSpec(memory_space=pl.ANY)] * 6,
        out_specs=pl.BlockSpec(memory_space=pltpu.VMEM),
        scratch_shapes=[
            vmem((1, TOK), I32),
            vmem((1, 128), I32),
            vmem((TOK, FEAT), BF16),
            vmem((FEAT, NZ * COLS), BF16),
            vmem((HELD, FEAT, RANK2), BF16),
            vmem((NY, NX, NC, HELD, RANK2 // 2, COLS), BF16),
            vmem((NA, MSG, FEAT), BF16),
            vmem((NA, MSG, FEAT), BF16),
            vmem((NA, MSG, RANK2), BF16),
            vmem((NA, MSG, RANK2), BF16),
            vmem((NY, TOK, ROWS), BF16),
            vmem((NZ, 16, RANK2), BF16),
            vmem((NZ - 1, 16, RANK2), BF16),
            vmem((16, RANK2), BF16),
            vmem((8, 16, RANK2), BF16),
            vmem((len(LEAVES), TOK, COLS), BF16),
            vmem((5, TOK, COLS), F32),
            vmem((len(LEAVES), TOK, COLS), BF16),
            vmem((4, TOK + 16, COLS), jnp.int16),
            vmem((4, TOK + 16, COLS), jnp.int16),
            dma((6,)),
            dma,
            dma,
            dma((NY,)),
            dma,
            dma((NY,)),
            dma,
            dma,
            dma,
            dma,
            dma,
            dma((5,)),
            dma,
            dma((4,)),
            dma((3,)),
            dma((3,)),
            pltpu.SemaphoreType.REGULAR,
            pltpu.SemaphoreType.REGULAR,
        ],
        compiler_params=pltpu.CompilerParams(
            collective_id=0, has_side_effects=True, vmem_limit_bytes=60 << 20
        ),
        name="lora_kv",
    )
    return call(
        token_adapter_index.reshape(1, TOK),
        adapter_table_row.reshape(1, 128),
        tokens,
        kv_weight,
        down_weight,
        up_weight,
    )


def solution(mesh):
    return jax.shard_map(
        per_device,
        mesh=mesh,
        in_specs=(
            P("adapter", "tensor"),
            P("adapter", None),
            P(),
            P("tensor", None),
            P("adapter", "tensor", None),
            P("adapter", None, None),
        ),
        out_specs=P("adapter", "tensor"),
        check_vma=False,
    )
```

```python
import jax
import jax.numpy as jnp
from jax import lax
from jax.experimental import pallas as pl
from jax.experimental.pallas import tpu as pltpu
from jax.sharding import PartitionSpec as P

CENTRES = (6, -6, 3, -3, 0)
LEAVES = ((0, 2), (0, 1), (0, -1), (1, 1), (1, -1), (2, 1), (2, -1), (3, 1), (3, -1), (4, 1), (4, -1))
WINDOWS = ((0, 1), (2,), (3,), (4,))

adapter_scale = 0.5
MESH = pl.DeviceIdType.MESH
F32, BF16, I32 = jnp.float32, jnp.bfloat16, jnp.int32

NY, NX, NC, NZ = 4, 4, 2, 16
NA = NY * NX * NC
TOK, FEAT, COLS = 256, 512, 128
HELD, CAP, RANK2 = 4, 8, 128
MSG = HELD * CAP
GROUP = NX * NC
ROWS = GROUP * MSG
OFFSETS = sorted(
    ((dy, dx, dc) for dy in range(NY) for dx in range(NX) for dc in range(NC)),
    key=lambda o: (-min(o[0], NY - o[0]) - min(o[1], NX - o[1]), -o[2], o[0], o[1]),
)
GROUPS = [OFFSETS[i : i + GROUP] for i in range(0, NA, GROUP)]
SELF = NA - 1


def iota(shape, dim):
    return lax.broadcasted_iota(I32, shape, dim)


def dot(a, b):
    return jnp.dot(a, b, preferred_element_type=F32)


def kernel(
    ids_hbm, table_hbm, tokens_hbm, kv_hbm, down_hbm, up_hbm, out_ref,
    ids, names_row, tok, kv, down, up, sbuf, rbuf, lbuf, ret, place, zsend, zrecv, zown, pack,
    b1, own, r1, w2, r2,
    load_sem, self_sem, tok_send, tok_recv, ret_send, ret_recv, zs_send, zs_recv, zg_send, zg_recv,
    l1_send, l1_recv, l2_send, l2_recv, up_send, up_recv, far_sem, farther_sem,
):
    a, z = lax.axis_index("adapter"), lax.axis_index("tensor")
    y, x, c = lax.div(a, GROUP), lax.rem(lax.div(a, NC), NX), lax.rem(a, NC)
    pend = {}

    def at(dy, dx, dc):
        return (
            lax.rem(y + dy + NY, NY) * GROUP + lax.rem(x + dx + NX, NX) * NC + lax.rem(c + dc + NC, NC)
        )

    def along_z(dz):
        return lax.rem(z + dz + NZ, NZ)

    def plane_copy(src, dst, send, recv, peer):
        return pltpu.make_async_remote_copy(
            src, dst, send, recv, device_id={"adapter": peer}, device_id_type=MESH
        )

    def z_copy(src, dst, send, recv, peer):
        return pltpu.make_async_remote_copy(
            src, dst, send, recv, device_id={"tensor": peer}, device_id_type=MESH
        )

    def wait_bytes(ref, sem):
        pltpu.make_async_copy(ref, ref, sem).wait()

    def later(name, ref, sem):
        pend[name] = (ref, sem)

    def due(name):
        wait_bytes(*pend.pop(name))

    def signal_z(sem, dz):
        pl.semaphore_signal(sem, 1, device_id={"tensor": along_z(dz)}, device_id_type=MESH)

    loads = [
        pltpu.make_async_copy(ids_hbm, ids, load_sem.at[4]),
        pltpu.make_async_copy(table_hbm, names_row, load_sem.at[5]),
        pltpu.make_async_copy(tokens_hbm, tok, load_sem.at[0]),
        pltpu.make_async_copy(kv_hbm, kv, load_sem.at[1]),
        pltpu.make_async_copy(down_hbm, down, load_sem.at[2]),
        pltpu.make_async_copy(
            up_hbm.at[:, :, pl.ds(pl.multiple_of(z * COLS, COLS), COLS)], up.at[y, x, c], load_sem.at[3]
        ),
    ]
    for load in loads:
        load.start()

    barrier = pltpu.get_barrier_semaphore()

    for offset in OFFSETS[:SELF]:
        pl.semaphore_signal(barrier, 1, device_id={"adapter": at(*offset)}, device_id_type=MESH)

    for dz in (1, -1, 2, -2):
        signal_z(barrier, dz)

    names = iota((128, TOK), 0)
    loads[0].wait()
    loads[1].wait()
    table = jnp.broadcast_to(names_row[...].astype(F32), (8, 128)).astype(BF16)
    hit = (names == ids[...]).astype(F32)
    square0, square1 = iota((TOK, TOK), 0), iota((TOK, TOK), 1)
    row = dot(table, hit.astype(BF16))[0:1]
    earlier = dot(hit.astype(BF16), (square0 < square1).astype(F32).astype(BF16))
    within = jnp.sum(hit * earlier, axis=0, keepdims=True)
    slot = row.astype(I32) * CAP + within.astype(I32)

    def firsts(g):
        return [at(*offset) * MSG for offset in GROUPS[g]]

    def remote(g):
        return slice(g * GROUP, min(g * GROUP + GROUP, SELF))

    def part(dz):
        d = along_z(dz)
        return dot(tok[...], kv[:, pl.ds(pl.multiple_of(d * COLS, COLS), COLS)])

    loads[2].wait()
    half = TOK // 2
    def leaves(turn):
        for w in WINDOWS[turn]:
            for dz in (2, 1, -1) if w == 0 else (1, -1):
                k = LEAVES.index((w, dz))
                b1[k] = part(dz + CENTRES[w]).astype(BF16)
                z_copy(b1.at[k], r1.at[k], l1_send, l1_recv.at[w], along_z(dz)).start()
            k = LEAVES.index((w, 1))
            later(f"l1{w}", r1.at[0:3] if w == 0 else r1.at[k : k + 2], l1_recv.at[w])
    message = iota((MSG, TOK), 0)
    for turn in range(len(GROUPS)):
        chosen = jnp.concatenate([(message == slot - first).astype(F32) for first in firsts(turn)], axis=0)
        sbuf[turn * GROUP : (turn + 1) * GROUP] = dot(chosen.astype(BF16), tok[...]).astype(BF16).reshape(GROUP, MSG, FEAT)
        if turn == 0:
            pl.semaphore_wait(barrier, NA - 1 + 4)
            signal_z(far_sem, 2)
            signal_z(far_sem, -2)
        for i, offset in enumerate(GROUPS[turn]):
            k = turn * GROUP + i
            if k == SELF:
                copy = pltpu.make_async_copy(sbuf.at[k], rbuf.at[k], self_sem)
                later("self", sbuf.at[k], self_sem)
            else:
                copy = plane_copy(sbuf.at[k], rbuf.at[k], tok_send, tok_recv.at[turn], at(*offset))
            copy.start()
        later(f"tok{turn}", rbuf.at[remote(turn)], tok_recv.at[turn])
    loads[3].wait()
    for turn in range(4): leaves(turn)
    later("tok_send", sbuf.at[0:SELF], tok_send)
    later("l1_send", b1, l1_send)
    for w in range(5):
        own[w] = part(CENTRES[w])
    pl.semaphore_wait(far_sem, 2)
    signal_z(farther_sem, 4)
    signal_z(farther_sem, -4)

    loads[5].wait()

    def first_axis(k):
        return jnp.where(c == 0, at(0, k, 0), at(k, 0, 0))

    diagonal = square0 == square1
    ones = jnp.ones((TOK, 128), BF16)
    row_at = dot(jnp.where(diagonal, row, 0.0).astype(BF16), ones)
    within_at = dot(jnp.where(diagonal, within, 0.0).astype(BF16), ones)
    slot_at = (row_at * CAP + within_at).astype(I32)
    slot_at = jnp.concatenate([slot_at, slot_at], axis=1)
    lane = iota((8, ROWS), 1)
    for g in range(len(GROUPS)):
        slots = lane & (MSG - 1)
        for i, first in enumerate(firsts(g)):
            slots += jnp.where((lane >> 5) == i, first, 0)
        place[g] = (slots[0:1] == slot_at).astype(F32).astype(BF16)

    loads[4].wait()
    left = jnp.concatenate([down[0], down[1]], axis=1)
    right = jnp.concatenate([down[2], down[3]], axis=1)
    which = (iota((ROWS, RANK2), 0) >> 3) & (HELD - 1)
    def window(w):
        due(f"l1{w}")
        k = LEAVES.index((w, 1))
        total = own[w] + r1[k].astype(F32) + r1[k + 1].astype(F32)
        return total + r1[0].astype(F32) if w == 0 else total

    def encode(w, total):
        most = jnp.max(jnp.max(jnp.abs(total), axis=0, keepdims=True), axis=1, keepdims=True)
        power = jnp.ceil(jnp.log2(jnp.maximum(most, 1e-30)) + 0.01)
        w2[w, 0:TOK] = jnp.round(total * (32000.0 * jnp.exp2(-power))).astype(I32).astype(jnp.int16)
        w2[w, TOK : TOK + 16] = jnp.broadcast_to(power, (16, COLS)).astype(I32).astype(jnp.int16)

    def decode(w):
        power = r2[w, TOK : TOK + 16].astype(I32).astype(F32)[0:1]
        return r2[w, 0:TOK].astype(I32).astype(F32) * (jnp.exp2(power) * (1 / 32000.0))

    def outer(w):
        encode(w, window(w))
        z_copy(w2.at[w], r2.at[w], l2_send, l2_recv.at[w], along_z(CENTRES[w] // 2)).start()
        later(f"l2{w}", r2.at[w], l2_recv.at[w])

    def inner(w):
        due(f"l2{w - 2}")
        encode(w, window(w) + decode(w - 2))
        z_copy(w2.at[w], r2.at[w], l2_send, l2_recv.at[w], along_z(CENTRES[w])).start()
        later(f"l2{w}", r2.at[w], l2_recv.at[w])

    def root():
        total = window(4)
        due("l22")
        due("l23")
        own[4] = total + decode(2) + decode(3)

    def token_step(g):
        lo = g * GROUP
        due(f"tok{g}")
        if g == len(GROUPS) - 1:
            due("self")
        arrived = rbuf[lo : lo + GROUP].reshape(ROWS, FEAT)
        l01, l23 = dot(arrived, left), dot(arrived, right)
        low_rank = jnp.where(
            which < 2,
            jnp.where(which == 0, l01[:, :RANK2], l01[:, RANK2:]),
            jnp.where(which == 2, l23[:, :RANK2], l23[:, RANK2:]),
        ).astype(BF16)
        lbuf[lo : lo + GROUP] = low_rank.reshape(GROUP, MSG, RANK2)
        for i, (dy, dx, dc) in enumerate(GROUPS[g]):
            k = lo + i
            if k == SELF:
                ret[k] = lbuf[k]
            else:
                plane_copy(lbuf.at[k], ret.at[k], ret_send, ret_recv.at[g], at(-dy, -dx, -dc)).start()
        later(f"ret{g}", ret.at[remote(g)], ret_recv.at[g])

    token_step(0)
    outer(0)
    outer(1)
    token_step(1)
    token_step(2)
    token_step(3)
    later("l2_send", w2, l2_send)
    later("ret_send", lbuf.at[0:SELF], ret_send)

    for k in (2, 1, 3):
        plane_copy(up.at[y, x, c], up.at[y, x, c], up_send.at[0], up_recv.at[0], first_axis(k)).start()
    later("up0", up.at[0, 0:3, 0], up_recv.at[0])
    later("up_send0", up.at[0, 0:3, 0], up_send.at[0])

    low_rank = jnp.zeros((TOK, RANK2), F32)
    for g in range(len(GROUPS)):
        due(f"ret{g}")
        low_rank += dot(place[g], ret[g * GROUP : (g + 1) * GROUP].reshape(ROWS, RANK2))
    upper, lower = low_rank[:half], low_rank[half:]
    first_lanes = iota((half, RANK2), 1) < RANK2 // 2
    keys = jnp.where(first_lanes, upper, pltpu.roll(lower, RANK2 // 2, 1))
    values = jnp.where(first_lanes, pltpu.roll(upper, RANK2 // 2, 1), lower)
    zsend[0:8] = keys.astype(BF16).reshape(8, 16, RANK2)
    zsend[8:16] = values.astype(BF16).reshape(8, 16, RANK2)
    pl.semaphore_wait(farther_sem, 2)
    for k in (8, 7, 9, 6, 10, 5, 11, 4, 12, 3, 13, 2, 14, 1, 15):
        z_copy(zsend.at[along_z(k + 4 - NZ)], zrecv.at[k - 1], zs_send, zs_recv, along_z(k)).start()
    later("zs", zrecv, zs_recv)
    later("zs_send", zrecv, zs_send)

    inner(2)
    inner(3)
    due("up0")

    @pl.when(c == 0)
    def _():
        for k in (2, 1, 3):
            plane_copy(up.at[y, :, 0], up.at[y, :, 0], up_send.at[1], up_recv.at[1], at(k, 0, 0)).start()

    @pl.when(c == 1)
    def _():
        for k in (2, 1, 3):
            plane_copy(up.at[:, x, 1], up.at[:, x, 1], up_send.at[1], up_recv.at[1], at(0, k, 0)).start()
    later("up1", up.at[0:3, :, 0], up_recv.at[1])
    later("up_send1", up.at[0:3, :, 0], up_send.at[1])

    due("zs")
    mine = along_z(4)
    total = zsend[mine].astype(F32)
    for k in range(NZ - 1):
        total += zrecv[k].astype(F32)
    spot, side, spot_z = lax.rem(mine, 8), lax.div(mine, 8) * 8, lax.rem(z, 8)
    zown[...] = total.astype(BF16)

    @pl.when(spot >= 4)
    def _():
        pack[spot] = zown[...]

    for t in (0, 1, 2, 3, 7, 6, 5, 4):

        @pl.when(spot != t + 4)
        def _(t=t):
            z_copy(zown, pack.at[spot], zg_send, zg_recv, side + t).start()

    due("up1")
    other = at(0, 0, 1)
    plane_copy(up.at[:, :, c], up.at[:, :, c], up_send.at[2], up_recv.at[2], other).start()
    later("up2", up.at[:, :, 0], up_recv.at[2])
    later("up_send2", up.at[:, :, 0], up_send.at[2])

    root()

    @pl.when(spot_z < 4)
    def _():
        wait_bytes(pack.at[0:7], zg_recv)

    @pl.when(spot_z >= 4)
    def _():
        wait_bytes(pack, zg_recv)

    due("up2")

    full = pack[...].reshape(half, RANK2).astype(F32)
    turned = pltpu.roll(full, RANK2 // 2, 1)
    twice = jnp.concatenate(
        [jnp.where(first_lanes, full, turned), jnp.where(first_lanes, turned, full)], axis=0
    ).astype(BF16)
    twice = jnp.concatenate([twice, twice], axis=1)
    half_of = iota((TOK, 256), 1) >> 6
    shifted = jnp.concatenate([row_at, row_at], axis=1).astype(I32) - half_of
    delta = jnp.zeros((TOK, COLS), F32)
    for h in range(NA):
        block = jnp.where(shifted == HELD * h, twice, jnp.zeros_like(twice))
        delta += dot(block, up[h // GROUP, h // NC % NX, h % NC].reshape(HELD * 64, COLS))
    result = own[4] + adapter_scale * delta
    out_ref[...] = result.astype(BF16)

    @pl.when(spot < 4)
    def _():
        wait_bytes(pack, zg_send)

    @pl.when(spot >= 4)
    def _():
        wait_bytes(pack.at[0:7], zg_send)

    for n in list(pend):
        due(n)


def per_device(tokens, token_adapter_index, adapter_table_row, kv_weight, down_weight, up_weight):
    dma = pltpu.SemaphoreType.DMA
    vmem = pltpu.VMEM
    call = pl.pallas_call(
        kernel,
        out_shape=jax.ShapeDtypeStruct((TOK, COLS), BF16),
        in_specs=[pl.BlockSpec(memory_space=pl.ANY)] * 6,
        out_specs=pl.BlockSpec(memory_space=pltpu.VMEM),
        scratch_shapes=[
            vmem((1, TOK), I32),
            vmem((1, 128), I32),
            vmem((TOK, FEAT), BF16),
            vmem((FEAT, NZ * COLS), BF16),
            vmem((HELD, FEAT, RANK2), BF16),
            vmem((NY, NX, NC, HELD, RANK2 // 2, COLS), BF16),
            vmem((NA, MSG, FEAT), BF16),
            vmem((NA, MSG, FEAT), BF16),
            vmem((NA, MSG, RANK2), BF16),
            vmem((NA, MSG, RANK2), BF16),
            vmem((NY, TOK, ROWS), BF16),
            vmem((NZ, 16, RANK2), BF16),
            vmem((NZ - 1, 16, RANK2), BF16),
            vmem((16, RANK2), BF16),
            vmem((8, 16, RANK2), BF16),
            vmem((len(LEAVES), TOK, COLS), BF16),
            vmem((5, TOK, COLS), F32),
            vmem((len(LEAVES), TOK, COLS), BF16),
            vmem((4, TOK + 16, COLS), jnp.int16),
            vmem((4, TOK + 16, COLS), jnp.int16),
            dma((6,)),
            dma,
            dma,
            dma((NY,)),
            dma,
            dma((NY,)),
            dma,
            dma,
            dma,
            dma,
            dma,
            dma((5,)),
            dma,
            dma((4,)),
            dma((3,)),
            dma((3,)),
            pltpu.SemaphoreType.REGULAR,
            pltpu.SemaphoreType.REGULAR,
        ],
        compiler_params=pltpu.CompilerParams(
            collective_id=0, has_side_effects=True, vmem_limit_bytes=60 << 20
        ),
        name="lora_kv",
    )
    return call(
        token_adapter_index.reshape(1, TOK),
        adapter_table_row.reshape(1, 128),
        tokens,
        kv_weight,
        down_weight,
        up_weight,
    )


def solution(mesh):
    return jax.shard_map(
        per_device,
        mesh=mesh,
        in_specs=(
            P("adapter", "tensor"),
            P("adapter", None),
            P(),
            P("tensor", None),
            P("adapter", "tensor", None),
            P("adapter", None, None),
        ),
        out_specs=P("adapter", "tensor"),
        check_vma=False,
    )
```

```python
import jax
import jax.numpy as jnp
from jax import lax
from jax.experimental import pallas as pl
from jax.experimental.pallas import tpu as pltpu
from jax.sharding import PartitionSpec as P

CENTRES = (6, -6, 3, -3, 0)
LEAVES = ((0, 2), (0, 1), (0, -1), (1, 1), (1, -1), (2, 1), (2, -1), (3, 1), (3, -1), (4, 1), (4, -1))
WINDOWS = ((0, 1), (2,), (3,), (4,))

adapter_scale = 0.5
MESH = pl.DeviceIdType.MESH
F32, BF16, I32 = jnp.float32, jnp.bfloat16, jnp.int32

NY, NX, NC, NZ = 4, 4, 2, 16
NA = NY * NX * NC
TOK, FEAT, COLS = 256, 512, 128
HELD, CAP, RANK2 = 4, 8, 128
MSG = HELD * CAP
GROUP = NX * NC
ROWS = GROUP * MSG
OFFSETS = sorted(
    ((dy, dx, dc) for dy in range(NY) for dx in range(NX) for dc in range(NC)),
    key=lambda o: (-min(o[0], NY - o[0]) - min(o[1], NX - o[1]), -o[2], o[0], o[1]),
)
GROUPS = [OFFSETS[i : i + GROUP] for i in range(0, NA, GROUP)]
SELF = NA - 1


def iota(shape, dim):
    return lax.broadcasted_iota(I32, shape, dim)


def dot(a, b):
    return jnp.dot(a, b, preferred_element_type=F32)


def kernel(
    ids_hbm, tokens_hbm, kv_hbm, down_hbm, up_hbm, out_ref,
    ids, names_row, tok, kv, down, up, sbuf, rbuf, lbuf, ret, place, zsend, zrecv, zown, pack,
    b1, own, r1, w2, r2,
    load_sem, self_sem, tok_send, tok_recv, ret_send, ret_recv, zs_send, zs_recv, zg_send, zg_recv,
    l1_send, l1_recv, l2_send, l2_recv, up_send, up_recv, far_sem, farther_sem,
):
    a, z = lax.axis_index("adapter"), lax.axis_index("tensor")
    y, x, c = lax.div(a, GROUP), lax.rem(lax.div(a, NC), NX), lax.rem(a, NC)
    pend = {}

    def at(dy, dx, dc):
        return (
            lax.rem(y + dy + NY, NY) * GROUP + lax.rem(x + dx + NX, NX) * NC + lax.rem(c + dc + NC, NC)
        )

    def along_z(dz):
        return lax.rem(z + dz + NZ, NZ)

    def plane_copy(src, dst, send, recv, peer):
        return pltpu.make_async_remote_copy(
            src, dst, send, recv, device_id={"adapter": peer}, device_id_type=MESH
        )

    def z_copy(src, dst, send, recv, peer):
        return pltpu.make_async_remote_copy(
            src, dst, send, recv, device_id={"tensor": peer}, device_id_type=MESH
        )

    def wait_bytes(ref, sem):
        pltpu.make_async_copy(ref, ref, sem).wait()

    def later(name, ref, sem):
        pend[name] = (ref, sem)

    def due(name):
        wait_bytes(*pend.pop(name))

    def signal_z(sem, dz):
        pl.semaphore_signal(sem, 1, device_id={"tensor": along_z(dz)}, device_id_type=MESH)

    loads = [
        pltpu.make_async_copy(ids_hbm.at[:, :TOK], ids, load_sem.at[4]),
        pltpu.make_async_copy(ids_hbm.at[:, TOK:], names_row, load_sem.at[5]),
        pltpu.make_async_copy(tokens_hbm, tok, load_sem.at[0]),
        pltpu.make_async_copy(kv_hbm, kv, load_sem.at[1]),
        pltpu.make_async_copy(down_hbm, down, load_sem.at[2]),
        pltpu.make_async_copy(
            up_hbm.at[:, :, pl.ds(pl.multiple_of(z * COLS, COLS), COLS)], up.at[y, x, c], load_sem.at[3]
        ),
    ]
    for load in loads:
        load.start()

    barrier = pltpu.get_barrier_semaphore()

    for offset in OFFSETS[:SELF]:
        pl.semaphore_signal(barrier, 1, device_id={"adapter": at(*offset)}, device_id_type=MESH)

    for dz in (1, -1, 2, -2):
        signal_z(barrier, dz)

    names = iota((128, TOK), 0)
    loads[0].wait()
    loads[1].wait()
    table = jnp.broadcast_to(names_row[...].astype(F32), (8, 128)).astype(BF16)
    hit = (names == ids[...]).astype(F32)
    square0, square1 = iota((TOK, TOK), 0), iota((TOK, TOK), 1)
    row = dot(table, hit.astype(BF16))[0:1]
    earlier = dot(hit.astype(BF16), (square0 < square1).astype(F32).astype(BF16))
    within = jnp.sum(hit * earlier, axis=0, keepdims=True)
    slot = row.astype(I32) * CAP + within.astype(I32)

    def firsts(g):
        return [at(*offset) * MSG for offset in GROUPS[g]]

    def remote(g):
        return slice(g * GROUP, min(g * GROUP + GROUP, SELF))

    def part(dz):
        d = along_z(dz)
        return dot(tok[...], kv[:, pl.ds(pl.multiple_of(d * COLS, COLS), COLS)])

    loads[2].wait()
    half = TOK // 2
    def leaves(turn):
        for w in WINDOWS[turn]:
            for dz in (2, 1, -1) if w == 0 else (1, -1):
                k = LEAVES.index((w, dz))
                b1[k] = part(dz + CENTRES[w]).astype(BF16)
                z_copy(b1.at[k], r1.at[k], l1_send, l1_recv.at[w], along_z(dz)).start()
            k = LEAVES.index((w, 1))
            later(f"l1{w}", r1.at[0:3] if w == 0 else r1.at[k : k + 2], l1_recv.at[w])
    message = iota((MSG, TOK), 0)
    for turn in range(len(GROUPS)):
        chosen = jnp.concatenate([(message == slot - first).astype(F32) for first in firsts(turn)], axis=0)
        sbuf[turn * GROUP : (turn + 1) * GROUP] = dot(chosen.astype(BF16), tok[...]).astype(BF16).reshape(GROUP, MSG, FEAT)
        if turn == 0:
            pl.semaphore_wait(barrier, NA - 1 + 4)
            signal_z(far_sem, 2)
            signal_z(far_sem, -2)
        for i, offset in enumerate(GROUPS[turn]):
            k = turn * GROUP + i
            if k == SELF:
                copy = pltpu.make_async_copy(sbuf.at[k], rbuf.at[k], self_sem)
                later("self", sbuf.at[k], self_sem)
            else:
                copy = plane_copy(sbuf.at[k], rbuf.at[k], tok_send, tok_recv.at[turn], at(*offset))
            copy.start()
        later(f"tok{turn}", rbuf.at[remote(turn)], tok_recv.at[turn])
    loads[3].wait()
    for turn in range(4): leaves(turn)
    later("tok_send", sbuf.at[0:SELF], tok_send)
    later("l1_send", b1, l1_send)
    for w in range(5):
        own[w] = part(CENTRES[w])
    pl.semaphore_wait(far_sem, 2)
    signal_z(farther_sem, 4)
    signal_z(farther_sem, -4)

    loads[5].wait()

    def first_axis(k):
        return jnp.where(c == 0, at(0, k, 0), at(k, 0, 0))

    diagonal = square0 == square1
    ones = jnp.ones((TOK, 128), BF16)
    row_at = dot(jnp.where(diagonal, row, 0.0).astype(BF16), ones)
    within_at = dot(jnp.where(diagonal, within, 0.0).astype(BF16), ones)
    slot_at = (row_at * CAP + within_at).astype(I32)
    slot_at = jnp.concatenate([slot_at, slot_at], axis=1)
    lane = iota((8, ROWS), 1)
    for g in range(len(GROUPS)):
        slots = lane & (MSG - 1)
        for i, first in enumerate(firsts(g)):
            slots += jnp.where((lane >> 5) == i, first, 0)
        place[g] = (slots[0:1] == slot_at).astype(F32).astype(BF16)

    loads[4].wait()
    left = jnp.concatenate([down[0], down[1]], axis=1)
    right = jnp.concatenate([down[2], down[3]], axis=1)
    which = (iota((ROWS, RANK2), 0) >> 3) & (HELD - 1)
    def window(w):
        due(f"l1{w}")
        k = LEAVES.index((w, 1))
        total = own[w] + r1[k].astype(F32) + r1[k + 1].astype(F32)
        return total + r1[0].astype(F32) if w == 0 else total

    def encode(w, total):
        most = jnp.max(jnp.max(jnp.abs(total), axis=0, keepdims=True), axis=1, keepdims=True)
        power = jnp.ceil(jnp.log2(jnp.maximum(most, 1e-30)) + 0.01)
        w2[w, 0:TOK] = jnp.round(total * (32000.0 * jnp.exp2(-power))).astype(I32).astype(jnp.int16)
        w2[w, TOK : TOK + 16] = jnp.broadcast_to(power, (16, COLS)).astype(I32).astype(jnp.int16)

    def decode(w):
        power = r2[w, TOK : TOK + 16].astype(I32).astype(F32)[0:1]
        return r2[w, 0:TOK].astype(I32).astype(F32) * (jnp.exp2(power) * (1 / 32000.0))

    def outer(w):
        encode(w, window(w))
        z_copy(w2.at[w], r2.at[w], l2_send, l2_recv.at[w], along_z(CENTRES[w] // 2)).start()
        later(f"l2{w}", r2.at[w], l2_recv.at[w])

    def inner(w):
        due(f"l2{w - 2}")
        encode(w, window(w) + decode(w - 2))
        z_copy(w2.at[w], r2.at[w], l2_send, l2_recv.at[w], along_z(CENTRES[w])).start()
        later(f"l2{w}", r2.at[w], l2_recv.at[w])

    def root():
        total = window(4)
        due("l22")
        due("l23")
        own[4] = total + decode(2) + decode(3)

    def token_step(g):
        lo = g * GROUP
        due(f"tok{g}")
        if g == len(GROUPS) - 1:
            due("self")
        arrived = rbuf[lo : lo + GROUP].reshape(ROWS, FEAT)
        l01, l23 = dot(arrived, left), dot(arrived, right)
        low_rank = jnp.where(
            which < 2,
            jnp.where(which == 0, l01[:, :RANK2], l01[:, RANK2:]),
            jnp.where(which == 2, l23[:, :RANK2], l23[:, RANK2:]),
        ).astype(BF16)
        lbuf[lo : lo + GROUP] = low_rank.reshape(GROUP, MSG, RANK2)
        for i, (dy, dx, dc) in enumerate(GROUPS[g]):
            k = lo + i
            if k == SELF:
                ret[k] = lbuf[k]
            else:
                plane_copy(lbuf.at[k], ret.at[k], ret_send, ret_recv.at[g], at(-dy, -dx, -dc)).start()
        later(f"ret{g}", ret.at[remote(g)], ret_recv.at[g])

    outer(0)
    outer(1)
    token_step(0)
    token_step(1)
    token_step(2)
    token_step(3)
    later("l2_send", w2, l2_send)
    later("ret_send", lbuf.at[0:SELF], ret_send)

    for k in (2, 1, 3):
        plane_copy(up.at[y, x, c], up.at[y, x, c], up_send.at[0], up_recv.at[0], first_axis(k)).start()
    later("up0", up.at[0, 0:3, 0], up_recv.at[0])
    later("up_send0", up.at[0, 0:3, 0], up_send.at[0])

    low_rank = jnp.zeros((TOK, RANK2), F32)
    for g in range(len(GROUPS)):
        due(f"ret{g}")
        low_rank += dot(place[g], ret[g * GROUP : (g + 1) * GROUP].reshape(ROWS, RANK2))
    upper, lower = low_rank[:half], low_rank[half:]
    first_lanes = iota((half, RANK2), 1) < RANK2 // 2
    keys = jnp.where(first_lanes, upper, pltpu.roll(lower, RANK2 // 2, 1))
    values = jnp.where(first_lanes, pltpu.roll(upper, RANK2 // 2, 1), lower)
    zsend[0:8] = keys.astype(BF16).reshape(8, 16, RANK2)
    zsend[8:16] = values.astype(BF16).reshape(8, 16, RANK2)
    pl.semaphore_wait(farther_sem, 2)
    for k in (8, 7, 9, 6, 10, 5, 11, 4, 12, 3, 13, 2, 14, 1, 15):
        z_copy(zsend.at[along_z(k + 4 - NZ)], zrecv.at[k - 1], zs_send, zs_recv, along_z(k)).start()
    later("zs", zrecv, zs_recv)
    later("zs_send", zrecv, zs_send)

    inner(2)
    inner(3)
    due("up0")

    @pl.when(c == 0)
    def _():
        for k in (2, 1, 3):
            plane_copy(up.at[y, :, 0], up.at[y, :, 0], up_send.at[1], up_recv.at[1], at(k, 0, 0)).start()

    @pl.when(c == 1)
    def _():
        for k in (2, 1, 3):
            plane_copy(up.at[:, x, 1], up.at[:, x, 1], up_send.at[1], up_recv.at[1], at(0, k, 0)).start()
    later("up1", up.at[0:3, :, 0], up_recv.at[1])
    later("up_send1", up.at[0:3, :, 0], up_send.at[1])

    due("zs")
    mine = along_z(4)
    total = zsend[mine].astype(F32)
    for k in range(NZ - 1):
        total += zrecv[k].astype(F32)
    spot, side, spot_z = lax.rem(mine, 8), lax.div(mine, 8) * 8, lax.rem(z, 8)
    zown[...] = total.astype(BF16)

    @pl.when(spot >= 4)
    def _():
        pack[spot] = zown[...]

    for t in (0, 1, 2, 3, 7, 6, 5, 4):

        @pl.when(spot != t + 4)
        def _(t=t):
            z_copy(zown, pack.at[spot], zg_send, zg_recv, side + t).start()

    due("up1")
    other = at(0, 0, 1)
    plane_copy(up.at[:, :, c], up.at[:, :, c], up_send.at[2], up_recv.at[2], other).start()
    later("up2", up.at[:, :, 0], up_recv.at[2])
    later("up_send2", up.at[:, :, 0], up_send.at[2])

    half_of = iota((TOK, 256), 1) >> 6
    shifted = jnp.concatenate([row_at, row_at], axis=1) - half_of.astype(F32)
    shifted = shifted.astype(BF16)

    root()

    @pl.when(spot_z < 4)
    def _():
        wait_bytes(pack.at[0:7], zg_recv)

    @pl.when(spot_z >= 4)
    def _():
        wait_bytes(pack, zg_recv)

    due("up2")

    full = pack[...].reshape(half, RANK2).astype(F32)
    turned = pltpu.roll(full, RANK2 // 2, 1)
    twice = jnp.concatenate(
        [jnp.where(first_lanes, full, turned), jnp.where(first_lanes, turned, full)], axis=0
    ).astype(BF16)
    twice = jnp.concatenate([twice, twice], axis=1)
    delta = jnp.zeros((TOK, COLS), F32)
    for h in range(NA):
        block = jnp.where(shifted == jnp.asarray(HELD * h, shifted.dtype), twice, jnp.zeros_like(twice))
        delta += dot(block, up[h // GROUP, h // NC % NX, h % NC].reshape(HELD * 64, COLS))
    result = own[4] + adapter_scale * delta
    out_ref[...] = result.astype(BF16)

    @pl.when(spot < 4)
    def _():
        wait_bytes(pack, zg_send)

    @pl.when(spot >= 4)
    def _():
        wait_bytes(pack.at[0:7], zg_send)

    for n in list(pend):
        due(n)


def per_device(tokens, token_adapter_index, adapter_table_row, kv_weight, down_weight, up_weight):
    dma = pltpu.SemaphoreType.DMA
    vmem = pltpu.VMEM
    call = pl.pallas_call(
        kernel,
        out_shape=jax.ShapeDtypeStruct((TOK, COLS), BF16),
        in_specs=[pl.BlockSpec(memory_space=pl.ANY)] * 5,
        out_specs=pl.BlockSpec(memory_space=pltpu.VMEM),
        scratch_shapes=[
            vmem((1, TOK), I32),
            vmem((1, 128), I32),
            vmem((TOK, FEAT), BF16),
            vmem((FEAT, NZ * COLS), BF16),
            vmem((HELD, FEAT, RANK2), BF16),
            vmem((NY, NX, NC, HELD, RANK2 // 2, COLS), BF16),
            vmem((NA, MSG, FEAT), BF16),
            vmem((NA, MSG, FEAT), BF16),
            vmem((NA, MSG, RANK2), BF16),
            vmem((NA, MSG, RANK2), BF16),
            vmem((NY, TOK, ROWS), BF16),
            vmem((NZ, 16, RANK2), BF16),
            vmem((NZ - 1, 16, RANK2), BF16),
            vmem((16, RANK2), BF16),
            vmem((8, 16, RANK2), BF16),
            vmem((len(LEAVES), TOK, COLS), BF16),
            vmem((5, TOK, COLS), F32),
            vmem((len(LEAVES), TOK, COLS), BF16),
            vmem((4, TOK + 16, COLS), jnp.int16),
            vmem((4, TOK + 16, COLS), jnp.int16),
            dma((6,)),
            dma,
            dma,
            dma((NY,)),
            dma,
            dma((NY,)),
            dma,
            dma,
            dma,
            dma,
            dma,
            dma((5,)),
            dma,
            dma((4,)),
            dma((3,)),
            dma((3,)),
            pltpu.SemaphoreType.REGULAR,
            pltpu.SemaphoreType.REGULAR,
        ],
        compiler_params=pltpu.CompilerParams(
            collective_id=0, has_side_effects=True, vmem_limit_bytes=55100 << 10
        ),
        name="lora_kv",
    )
    return call(
        jnp.concatenate([token_adapter_index.reshape(1, TOK), adapter_table_row.reshape(1, 128)], axis=1),
        tokens,
        kv_weight,
        down_weight,
        up_weight,
    )


def solution(mesh):
    return jax.shard_map(
        per_device,
        mesh=mesh,
        in_specs=(
            P("adapter", "tensor"),
            P("adapter", None),
            P(),
            P("tensor", None),
            P("adapter", "tensor", None),
            P("adapter", None, None),
        ),
        out_specs=P("adapter", "tensor"),
        check_vma=False,
    )
```

```python
import jax
import jax.numpy as jnp
from jax import lax
from jax.experimental import pallas as pl
from jax.experimental.pallas import tpu as pltpu
from jax.sharding import PartitionSpec as P

CENTRES = (6, -6, 3, -3, 0)
LEAVES = ((0, 2), (0, 1), (0, -1), (1, 1), (1, -1), (2, 1), (2, -1), (3, 1), (3, -1), (4, 1), (4, -1))
WINDOWS = ((0, 1), (2,), (3,), (4,))

adapter_scale = 0.5
MESH = pl.DeviceIdType.MESH
F32, BF16, I32 = jnp.float32, jnp.bfloat16, jnp.int32

NY, NX, NC, NZ = 4, 4, 2, 16
NA = NY * NX * NC
TOK, FEAT, COLS = 256, 512, 128
HELD, CAP, RANK2 = 4, 8, 128
MSG = HELD * CAP
GROUP = NX * NC
ROWS = GROUP * MSG
OFFSETS = sorted(
    ((dy, dx, dc) for dy in range(NY) for dx in range(NX) for dc in range(NC)),
    key=lambda o: (-min(o[0], NY - o[0]) - min(o[1], NX - o[1]), -o[2], o[0], o[1]),
)
GROUPS = [OFFSETS[i : i + GROUP] for i in range(0, NA, GROUP)]
SELF = NA - 1


def iota(shape, dim):
    return lax.broadcasted_iota(I32, shape, dim)


def dot(a, b):
    return jnp.dot(a, b, preferred_element_type=F32)


def kernel(
    ids_ref, tokens_hbm, kv_hbm, down_hbm, up_hbm, out_ref,
    tok, kv, down, up, sbuf, rbuf, lbuf, ret, place, zsend, zrecv, zown, pack,
    b1, own, r1, w2, r2,
    load_sem, self_sem, tok_send, tok_recv, ret_send, ret_recv, zs_send, zs_recv, zg_send, zg_recv,
    l1_send, l1_recv, l2_send, l2_recv, up_send, up_recv, far_sem, farther_sem,
):
    a, z = lax.axis_index("adapter"), lax.axis_index("tensor")
    y, x, c = lax.div(a, GROUP), lax.rem(lax.div(a, NC), NX), lax.rem(a, NC)
    pend = {}

    def at(dy, dx, dc):
        return (
            lax.rem(y + dy + NY, NY) * GROUP + lax.rem(x + dx + NX, NX) * NC + lax.rem(c + dc + NC, NC)
        )

    def along_z(dz):
        return lax.rem(z + dz + NZ, NZ)

    def plane_copy(src, dst, send, recv, peer):
        return pltpu.make_async_remote_copy(
            src, dst, send, recv, device_id={"adapter": peer}, device_id_type=MESH
        )

    def z_copy(src, dst, send, recv, peer):
        return pltpu.make_async_remote_copy(
            src, dst, send, recv, device_id={"tensor": peer}, device_id_type=MESH
        )

    def wait_bytes(ref, sem):
        pltpu.make_async_copy(ref, ref, sem).wait()

    def later(name, ref, sem):
        pend[name] = (ref, sem)

    def due(name):
        wait_bytes(*pend.pop(name))

    def signal_z(sem, dz):
        pl.semaphore_signal(sem, 1, device_id={"tensor": along_z(dz)}, device_id_type=MESH)

    loads = [
        pltpu.make_async_copy(tokens_hbm, tok, load_sem.at[0]),
        pltpu.make_async_copy(kv_hbm, kv, load_sem.at[1]),
        pltpu.make_async_copy(down_hbm, down, load_sem.at[2]),
        pltpu.make_async_copy(
            up_hbm.at[:, :, pl.ds(pl.multiple_of(z * COLS, COLS), COLS)], up.at[y, x, c], load_sem.at[3]
        ),
    ]
    for load in loads:
        load.start()

    barrier = pltpu.get_barrier_semaphore()

    for offset in OFFSETS[:SELF]:
        pl.semaphore_signal(barrier, 1, device_id={"adapter": at(*offset)}, device_id_type=MESH)

    for dz in (1, -1, 2, -2):
        signal_z(barrier, dz)

    names = iota((128, TOK), 0)
    table = jnp.broadcast_to(ids_ref[:, TOK:].astype(F32), (8, 128)).astype(BF16)
    hit = (names == ids_ref[:, :TOK]).astype(F32)
    square0, square1 = iota((TOK, TOK), 0), iota((TOK, TOK), 1)
    row = dot(table, hit.astype(BF16))[0:1]
    earlier = dot(hit.astype(BF16), (square0 < square1).astype(F32).astype(BF16))
    within = jnp.sum(hit * earlier, axis=0, keepdims=True)
    slot = row.astype(I32) * CAP + within.astype(I32)

    def firsts(g):
        return [at(*offset) * MSG for offset in GROUPS[g]]

    def remote(g):
        return slice(g * GROUP, min(g * GROUP + GROUP, SELF))

    def part(dz):
        d = along_z(dz)
        return dot(tok[...], kv[:, pl.ds(pl.multiple_of(d * COLS, COLS), COLS)])

    loads[0].wait()
    half = TOK // 2
    def leaves(turn):
        for w in WINDOWS[turn]:
            for dz in (2, 1, -1) if w == 0 else (1, -1):
                k = LEAVES.index((w, dz))
                b1[k] = part(dz + CENTRES[w]).astype(BF16)
                z_copy(b1.at[k], r1.at[k], l1_send, l1_recv.at[w], along_z(dz)).start()
            k = LEAVES.index((w, 1))
            later(f"l1{w}", r1.at[0:3] if w == 0 else r1.at[k : k + 2], l1_recv.at[w])
    message = iota((MSG, TOK), 0)
    def fill(turn):
        chosen = jnp.concatenate([(message == slot - first).astype(F32) for first in firsts(turn)], axis=0)
        sbuf[turn * GROUP : (turn + 1) * GROUP] = dot(chosen.astype(BF16), tok[...]).astype(BF16).reshape(GROUP, MSG, FEAT)

    fill(0)
    fill(1)
    for turn in range(len(GROUPS)):
        if turn > 1:
            fill(turn)
        if turn == 0:
            pl.semaphore_wait(barrier, NA - 1 + 4)
            signal_z(far_sem, 2)
            signal_z(far_sem, -2)
        for i, offset in enumerate(GROUPS[turn]):
            k = turn * GROUP + i
            if k == SELF:
                copy = pltpu.make_async_copy(sbuf.at[k], rbuf.at[k], self_sem)
                later("self", sbuf.at[k], self_sem)
            else:
                copy = plane_copy(sbuf.at[k], rbuf.at[k], tok_send, tok_recv.at[turn], at(*offset))
            copy.start()
        later(f"tok{turn}", rbuf.at[remote(turn)], tok_recv.at[turn])
    loads[1].wait()
    for turn in range(4): leaves(turn)
    later("tok_send", sbuf.at[0:SELF], tok_send)
    later("l1_send", b1, l1_send)
    for w in range(5):
        own[w] = part(CENTRES[w])
    pl.semaphore_wait(far_sem, 2)
    signal_z(farther_sem, 4)
    signal_z(farther_sem, -4)

    loads[3].wait()

    def first_axis(k):
        return jnp.where(c == 0, at(0, k, 0), at(k, 0, 0))

    diagonal = square0 == square1
    ones = jnp.ones((TOK, 128), BF16)
    row_at = dot(jnp.where(diagonal, row, 0.0).astype(BF16), ones)
    within_at = dot(jnp.where(diagonal, within, 0.0).astype(BF16), ones)
    slot_at = (row_at * CAP + within_at).astype(I32)
    slot_at = jnp.concatenate([slot_at, slot_at], axis=1)
    lane = iota((8, ROWS), 1)
    for g in range(len(GROUPS)):
        slots = lane & (MSG - 1)
        for i, first in enumerate(firsts(g)):
            slots += jnp.where((lane >> 5) == i, first, 0)
        place[g] = (slots[0:1] == slot_at).astype(F32).astype(BF16)

    loads[2].wait()
    left = jnp.concatenate([down[0], down[1]], axis=1)
    right = jnp.concatenate([down[2], down[3]], axis=1)
    which = (iota((ROWS, RANK2), 0) >> 3) & (HELD - 1)
    def window(w):
        due(f"l1{w}")
        k = LEAVES.index((w, 1))
        total = own[w] + r1[k].astype(F32) + r1[k + 1].astype(F32)
        return total + r1[0].astype(F32) if w == 0 else total

    def encode(w, total):
        most = jnp.max(jnp.max(jnp.abs(total), axis=0, keepdims=True), axis=1, keepdims=True)
        power = jnp.ceil(jnp.log2(jnp.maximum(most, 1e-30)) + 0.01)
        w2[w, 0:TOK] = jnp.round(total * (32000.0 * jnp.exp2(-power))).astype(I32).astype(jnp.int16)
        w2[w, TOK : TOK + 16] = jnp.broadcast_to(power, (16, COLS)).astype(I32).astype(jnp.int16)

    def decode(w):
        power = r2[w, TOK : TOK + 16].astype(I32).astype(F32)[0:1]
        return r2[w, 0:TOK].astype(I32).astype(F32) * (jnp.exp2(power) * (1 / 32000.0))

    def outer(w):
        encode(w, window(w))
        z_copy(w2.at[w], r2.at[w], l2_send, l2_recv.at[w], along_z(CENTRES[w] // 2)).start()
        later(f"l2{w}", r2.at[w], l2_recv.at[w])

    def inner(w):
        due(f"l2{w - 2}")
        encode(w, window(w) + decode(w - 2))
        z_copy(w2.at[w], r2.at[w], l2_send, l2_recv.at[w], along_z(CENTRES[w])).start()
        later(f"l2{w}", r2.at[w], l2_recv.at[w])

    def root():
        total = window(4)
        due("l22")
        due("l23")
        own[4] = total + decode(2) + decode(3)

    def token_step(g):
        lo = g * GROUP
        due(f"tok{g}")
        if g == len(GROUPS) - 1:
            due("self")
        arrived = rbuf[lo : lo + GROUP].reshape(ROWS, FEAT)
        l01, l23 = dot(arrived, left), dot(arrived, right)
        low_rank = jnp.where(
            which < 2,
            jnp.where(which == 0, l01[:, :RANK2], l01[:, RANK2:]),
            jnp.where(which == 2, l23[:, :RANK2], l23[:, RANK2:]),
        ).astype(BF16)
        lbuf[lo : lo + GROUP] = low_rank.reshape(GROUP, MSG, RANK2)
        for i, (dy, dx, dc) in enumerate(GROUPS[g]):
            k = lo + i
            if k == SELF:
                ret[k] = lbuf[k]
            else:
                plane_copy(lbuf.at[k], ret.at[k], ret_send, ret_recv.at[g], at(-dy, -dx, -dc)).start()
        later(f"ret{g}", ret.at[remote(g)], ret_recv.at[g])

    outer(0)
    outer(1)
    token_step(0)
    token_step(1)
    token_step(2)
    token_step(3)
    later("l2_send", w2, l2_send)
    later("ret_send", lbuf.at[0:SELF], ret_send)

    for k in (2, 1, 3):
        plane_copy(up.at[y, x, c], up.at[y, x, c], up_send.at[0], up_recv.at[0], first_axis(k)).start()
    later("up0", up.at[0, 0:3, 0], up_recv.at[0])
    later("up_send0", up.at[0, 0:3, 0], up_send.at[0])

    low_rank = jnp.zeros((TOK, RANK2), F32)
    for g in range(len(GROUPS)):
        due(f"ret{g}")
        low_rank += dot(place[g], ret[g * GROUP : (g + 1) * GROUP].reshape(ROWS, RANK2))
    upper, lower = low_rank[:half], low_rank[half:]
    first_lanes = iota((half, RANK2), 1) < RANK2 // 2
    keys = jnp.where(first_lanes, upper, pltpu.roll(lower, RANK2 // 2, 1))
    values = jnp.where(first_lanes, pltpu.roll(upper, RANK2 // 2, 1), lower)
    zsend[0:8] = keys.astype(BF16).reshape(8, 16, RANK2)
    zsend[8:16] = values.astype(BF16).reshape(8, 16, RANK2)
    pl.semaphore_wait(farther_sem, 2)
    for k in (8, 7, 9, 6, 10, 5, 11, 4, 12, 3, 13, 2, 14, 1, 15):
        z_copy(zsend.at[along_z(k + 4 - NZ)], zrecv.at[k - 1], zs_send, zs_recv, along_z(k)).start()
    later("zs", zrecv, zs_recv)
    later("zs_send", zrecv, zs_send)

    inner(2)
    inner(3)
    due("up0")

    @pl.when(c == 0)
    def _():
        for k in (2, 1, 3):
            plane_copy(up.at[y, :, 0], up.at[y, :, 0], up_send.at[1], up_recv.at[1], at(k, 0, 0)).start()

    @pl.when(c == 1)
    def _():
        for k in (2, 1, 3):
            plane_copy(up.at[:, x, 1], up.at[:, x, 1], up_send.at[1], up_recv.at[1], at(0, k, 0)).start()
    later("up1", up.at[0:3, :, 0], up_recv.at[1])
    later("up_send1", up.at[0:3, :, 0], up_send.at[1])

    due("zs")
    mine = along_z(4)
    total = zsend[mine].astype(F32)
    for k in range(NZ - 1):
        total += zrecv[k].astype(F32)
    spot, side, spot_z = lax.rem(mine, 8), lax.div(mine, 8) * 8, lax.rem(z, 8)
    zown[...] = total.astype(BF16)

    @pl.when(spot >= 4)
    def _():
        pack[spot] = zown[...]

    for t in (0, 1, 2, 3, 7, 6, 5, 4):

        @pl.when(spot != t + 4)
        def _(t=t):
            z_copy(zown, pack.at[spot], zg_send, zg_recv, side + t).start()

    due("up1")
    other = at(0, 0, 1)
    plane_copy(up.at[:, :, c], up.at[:, :, c], up_send.at[2], up_recv.at[2], other).start()
    later("up2", up.at[:, :, 0], up_recv.at[2])
    later("up_send2", up.at[:, :, 0], up_send.at[2])

    half_of = iota((TOK, 256), 1) >> 6
    shifted = jnp.concatenate([row_at, row_at], axis=1) - half_of.astype(F32)
    shifted = shifted.astype(BF16)

    root()

    @pl.when(spot_z < 4)
    def _():
        wait_bytes(pack.at[0:7], zg_recv)

    @pl.when(spot_z >= 4)
    def _():
        wait_bytes(pack, zg_recv)

    due("up2")

    full = pack[...].reshape(half, RANK2).astype(F32)
    turned = pltpu.roll(full, RANK2 // 2, 1)
    twice = jnp.concatenate(
        [jnp.where(first_lanes, full, turned), jnp.where(first_lanes, turned, full)], axis=0
    ).astype(BF16)
    twice = jnp.concatenate([twice, twice], axis=1)
    delta = jnp.zeros((TOK, COLS), F32)
    for h in range(NA):
        block = jnp.where(shifted == jnp.asarray(HELD * h, shifted.dtype), twice, jnp.zeros_like(twice))
        delta += dot(block, up[h // GROUP, h // NC % NX, h % NC].reshape(HELD * 64, COLS))
    result = own[4] + adapter_scale * delta
    out_ref[...] = result.astype(BF16)

    @pl.when(spot < 4)
    def _():
        wait_bytes(pack, zg_send)

    @pl.when(spot >= 4)
    def _():
        wait_bytes(pack.at[0:7], zg_send)

    for n in list(pend):
        due(n)


def per_device(tokens, token_adapter_index, adapter_table_row, kv_weight, down_weight, up_weight):
    dma = pltpu.SemaphoreType.DMA
    vmem = pltpu.VMEM
    call = pl.pallas_call(
        kernel,
        out_shape=jax.ShapeDtypeStruct((TOK, COLS), BF16),
        in_specs=[pl.BlockSpec(memory_space=pltpu.VMEM)] + [pl.BlockSpec(memory_space=pl.ANY)] * 4,
        out_specs=pl.BlockSpec(memory_space=pltpu.VMEM),
        scratch_shapes=[
            vmem((TOK, FEAT), BF16),
            vmem((FEAT, NZ * COLS), BF16),
            vmem((HELD, FEAT, RANK2), BF16),
            vmem((NY, NX, NC, HELD, RANK2 // 2, COLS), BF16),
            vmem((NA, MSG, FEAT), BF16),
            vmem((NA, MSG, FEAT), BF16),
            vmem((NA, MSG, RANK2), BF16),
            vmem((NA, MSG, RANK2), BF16),
            vmem((NY, TOK, ROWS), BF16),
            vmem((NZ, 16, RANK2), BF16),
            vmem((NZ - 1, 16, RANK2), BF16),
            vmem((16, RANK2), BF16),
            vmem((8, 16, RANK2), BF16),
            vmem((len(LEAVES), TOK, COLS), BF16),
            vmem((5, TOK, COLS), F32),
            vmem((len(LEAVES), TOK, COLS), BF16),
            vmem((4, TOK + 16, COLS), jnp.int16),
            vmem((4, TOK + 16, COLS), jnp.int16),
            dma((4,)),
            dma,
            dma,
            dma((NY,)),
            dma,
            dma((NY,)),
            dma,
            dma,
            dma,
            dma,
            dma,
            dma((5,)),
            dma,
            dma((4,)),
            dma((3,)),
            dma((3,)),
            pltpu.SemaphoreType.REGULAR,
            pltpu.SemaphoreType.REGULAR,
        ],
        compiler_params=pltpu.CompilerParams(
            collective_id=0, has_side_effects=True, vmem_limit_bytes=55100 << 10
        ),
        name="lora_kv",
    )
    return call(
        jnp.concatenate([token_adapter_index.reshape(1, TOK), adapter_table_row.reshape(1, 128)], axis=1),
        tokens,
        kv_weight,
        down_weight,
        up_weight,
    )


def solution(mesh):
    return jax.shard_map(
        per_device,
        mesh=mesh,
        in_specs=(
            P("adapter", "tensor"),
            P("adapter", None),
            P(),
            P("tensor", None),
            P("adapter", "tensor", None),
            P("adapter", None, None),
        ),
        out_specs=P("adapter", "tensor"),
        check_vma=False,
    )
```
